32 devices in a mesh: ctx: 8 (over y, x, core), fsdp: 4 (over z).
Axes of the slice: x: 2, y: 2, z: 4, core: 2. Of those that a mesh axis runs over, the one named last changes fastest.
Arguments:
- tokens: bfloat16 [4096, 4096], P(('ctx', 'fsdp')), may hold values from -360 to 360
- norm_gain: float32 [4096], replicated, may hold values from 0.1 to 1.9
- qkv_weight: bfloat16 [3, 4096, 2048], P(None, 'ctx', 'fsdp'), may hold values from -1 to 1
- out_weight: bfloat16 [2048, 4096], P('fsdp', 'ctx'), may hold values from -1 to 1
- layout: int32 [32, 16], replicated, may hold values from 0 to 31, as said below
Outputs:
- branch_out: bfloat16 [4096, 4096], P(('ctx', 'fsdp'))
The draws below stay inside these ranges and needn't reach their ends.
Inputs may be any that keep to these rules, and one draw needn't show every extreme that they name: `layout`: every entry of query block i names a block of 0 to i. With the blocks taken in spans of 4, the query blocks of one span name at most 2 distinct blocks of any other span, and some pair of spans reaches 2 in every draw.
All inputs are finite; a program needn't handle non-finite values.
Results may differ from the reference program's by a relative error of at most 0.015.
Values may be sent and summed in bfloat16 or wider, within the bound.
No kernel may reach another device: no remote copies, remote signals or barrier semaphores. Data moves between devices by JAX's collectives and lax.ppermute only.
A program may use at most 128 MiB of HBM per device.

```python
import math
import jax
import jax.numpy as jnp
from jax import lax

D = 4096
HEADS = 16
HEAD_DIM = 128
BLK = 128
SUMMARY = 16
CAP = 2
INNER = 2048
HEADS_DEV = 4
TOKENS = 4096
BLOCKS = 32
SPAN_BLOCKS = 4


def draw_tokens(key, part):
    subkeys = jax.random.split(key, 3)
    standard = jax.random.truncated_normal(subkeys[0], -3.0, 3.0, (TOKENS, D), jnp.float32)
    row_scale = jnp.exp(jax.random.uniform(subkeys[1], (TOKENS, 1), jnp.float32, 0.0, math.log(10.0)))
    column_scale = jnp.exp(jax.random.uniform(subkeys[2], (1, D), jnp.float32, 0.0, math.log(10.0)))
    return (standard * row_scale * column_scale).astype(jnp.bfloat16)


def draw_qkv_weight(key, part):
    subkeys = jax.random.split(key, 1)
    standard = jax.random.truncated_normal(subkeys[0], -4.0, 4.0, (3, D, INNER), jnp.float32) * D ** (-0.5)
    return standard.astype(jnp.bfloat16)


def draw_layout(key, part):
    subkeys = jax.random.split(key, 5)
    span_count = BLOCKS // SPAN_BLOCKS
    row_ids = jnp.arange(BLOCKS, dtype=jnp.int32)
    home_span = row_ids // SPAN_BLOCKS
    spread = jax.random.randint(subkeys[0], (span_count, span_count, SPAN_BLOCKS), 0, 1 << 20) * SPAN_BLOCKS + jnp.arange(SPAN_BLOCKS, dtype=jnp.int32)
    chosen = jnp.argsort(spread, axis=-1)[..., :CAP].astype(jnp.int32)
    source_span = jax.random.randint(subkeys[1], (BLOCKS, SUMMARY), 0, 1 << 20) % (home_span[:, None] + 1)
    pick_slot = jax.random.randint(subkeys[2], (BLOCKS, SUMMARY), 0, CAP)
    within = jax.random.randint(subkeys[3], (BLOCKS, SUMMARY), 0, 1 << 20) % (row_ids - home_span * SPAN_BLOCKS + 1)[:, None]
    remote = source_span * SPAN_BLOCKS + chosen[home_span[:, None], source_span, pick_slot]
    local_entry = home_span[:, None] * SPAN_BLOCKS + within
    entries = jnp.where(source_span == home_span[:, None], local_entry, remote)
    span_ids = jnp.arange(span_count, dtype=jnp.int32)
    forced_source = jax.random.randint(subkeys[4], (span_count,), 0, 1 << 20) % jnp.maximum(span_ids, 1)
    column_id = jnp.arange(SUMMARY, dtype=jnp.int32)
    forced = forced_source[:, None] * SPAN_BLOCKS + chosen[span_ids[:, None], forced_source[:, None], jnp.minimum(column_id, CAP - 1)[None, :]]
    override = (column_id[None, :] < CAP) & (span_ids[:, None] >= 1)
    first_rows = span_ids * SPAN_BLOCKS
    head_rows = entries[first_rows]
    entries = entries.at[first_rows].set(jnp.where(override, forced, head_rows))
    return entries.astype(jnp.int32)


def shard_levels(key, dims, shards, low, high):
    level = 1.0
    for axis_at, parts in shards:
        draws = jax.random.uniform(jax.random.fold_in(jax.random.fold_in(key, 6), axis_at), (parts,), jnp.float32, low / len(shards), high / len(shards))
        level = level * jnp.repeat(jnp.exp(draws), dims[axis_at] // parts).reshape((-1,) + (1,) * (len(dims) - 1 - axis_at))
    return level


def bell_draw(stream_key, shape, deviation, reach, cuts=(), held_as=jnp.bfloat16):
    drawn = jax.random.normal(stream_key, shape, jnp.float32) * deviation
    if len(cuts) > 0:
        drawn = shard_levels(stream_key, shape, cuts, -0.22, 0.18) * drawn
    return jnp.clip(drawn, min=-reach, max=reach).astype(held_as)


def setup_inputs(seed: int = 0) -> dict:
    key_of = jax.random.split(jax.random.key(seed), 6)
    return {
        "tokens": draw_tokens(jax.random.fold_in(key_of[5], 71), 0),
        "norm_gain": jnp.clip(1.0 + 0.18 * jax.random.normal(key_of[1], (D,), jnp.float32), 0.1, 1.9),
        "qkv_weight": draw_qkv_weight(jax.random.fold_in(key_of[5], 71), 0),
        "out_weight": bell_draw(key_of[3], (INNER, D), (INNER // 64) ** -0.5, 1.0, ((0, 4), (1, 8))),
        "layout": draw_layout(jax.random.fold_in(key_of[5], 71), 0),
    }


EPSILON = 1e-05

def normalize(tokens, norm_gain):
    features = tokens.astype(jnp.float32)
    mean_square = lax.optimization_barrier(jnp.mean(features * features, axis=-1, keepdims=True))
    return (features * lax.rsqrt(mean_square + EPSILON) * norm_gain).astype(jnp.bfloat16)

def reference(tokens, norm_gain, qkv_weight, out_weight, layout):
    normed = normalize(tokens, norm_gain)
    queries = lax.optimization_barrier(jnp.dot(normed, qkv_weight[0], preferred_element_type=jnp.float32).astype(jnp.bfloat16))
    key_rows = lax.optimization_barrier(jnp.dot(normed, qkv_weight[1], preferred_element_type=jnp.float32).astype(jnp.bfloat16))
    value_rows = lax.optimization_barrier(jnp.dot(normed, qkv_weight[2], preferred_element_type=jnp.float32).astype(jnp.bfloat16))
    block_count = TOKENS // BLK
    query_blocks = queries.reshape(block_count, BLK, INNER)
    key_blocks = key_rows.reshape(block_count, BLK, INNER)
    value_blocks = value_rows.reshape(block_count, BLK, INNER)
    key_slots = 2 + SUMMARY

    def one_block(block_id):
        block_id = block_id.astype(jnp.int32)
        key_index = jnp.concatenate([jnp.stack([block_id, block_id - 1]), layout[block_id]]).astype(jnp.int32)
        clipped = jnp.maximum(key_index, 0)
        slot_keys = key_blocks[clipped].astype(jnp.float32).reshape(key_slots, BLK, HEADS, HEAD_DIM)
        slot_values = value_blocks[clipped].astype(jnp.float32).reshape(key_slots, BLK, HEADS, HEAD_DIM)
        block_queries = query_blocks[block_id].astype(jnp.float32).reshape(BLK, HEADS, HEAD_DIM)
        scores = jnp.einsum('qhd,nkhd->hqnk', block_queries, slot_keys) * HEAD_DIM ** (-0.5)
        query_pos = block_id * BLK + jnp.arange(BLK, dtype=jnp.int32)
        key_pos = key_index[:, None] * BLK + jnp.arange(BLK, dtype=jnp.int32)[None, :]
        allowed = (key_pos[None, :, :] <= query_pos[:, None, None]) & (key_pos[None, :, :] >= 0)
        allowed = allowed[None]
        scores = jnp.where(allowed, scores, -1e+30)
        row_max = lax.optimization_barrier(jnp.max(scores, axis=(2, 3), keepdims=True))
        weights = jnp.where(allowed, jnp.exp(scores - row_max), 0.0)
        denominator = lax.optimization_barrier(jnp.sum(weights, axis=(2, 3), keepdims=True))
        weights = lax.optimization_barrier((weights / denominator).astype(jnp.bfloat16)).astype(jnp.float32)
        blended = jnp.einsum('hqnk,nkhd->qhd', weights, slot_values)
        return blended.reshape(BLK, INNER).astype(jnp.bfloat16)
    attended = lax.map(one_block, jnp.arange(block_count, dtype=jnp.int32)).reshape(TOKENS, INNER)
    span_width = HEADS_DEV * HEAD_DIM
    running = jnp.zeros((TOKENS, D), jnp.float32)
    for group_id in range(HEADS // HEADS_DEV):
        part_out = jnp.dot(attended[:, group_id * span_width:(group_id + 1) * span_width], out_weight[group_id * span_width:(group_id + 1) * span_width], preferred_element_type=jnp.float32)
        running = running + lax.optimization_barrier(part_out.astype(jnp.bfloat16)).astype(jnp.float32)
    return running.astype(jnp.bfloat16)
```

```python
import functools
import math

import jax
import jax.numpy as jnp
import numpy as np
from jax import lax
from jax.experimental import pallas as pl
from jax.experimental.pallas import tpu as pltpu
from jax.sharding import Mesh
from jax.sharding import PartitionSpec as P

HEAD_DIM = 128
BLK = 128
EPSILON = 1e-05
MASKED = -1e30
F32 = jnp.float32
BF16 = jnp.bfloat16


def xor_pairs(size, bit):
    return [(i, i ^ bit) for i in range(size)]


def line_order(size):
    if size != 4:
        return [list(range(size))] * size
    return [[0, 1, 2, 3], [1, 2, 3, 0], [2, 1, 0, 3], [3, 2, 1, 0]]


def line_gather(part, axis, size):
    if size != 4:
        whole = lax.all_gather(part, axis, axis=0)
        return [whole[i] for i in range(size)]
    low = lax.axis_index(axis) < 2
    up = lax.ppermute(part, axis, [(0, 1), (1, 2), (2, 3)])
    down = lax.ppermute(part, axis, [(1, 0), (2, 1), (3, 2)])
    up2 = lax.ppermute(up, axis, [(1, 2), (2, 3)])
    down2 = lax.ppermute(down, axis, [(2, 1), (1, 0)])
    second = jnp.where(low, down2, up2)
    ends = lax.ppermute(second, axis, [(2, 3), (1, 0)])
    near = jnp.where(low, down, up)
    inner = jnp.where(low, up, down)
    at = lax.axis_index(axis)
    last = jnp.where((at == 1) | (at == 2), inner, ends)
    return [part, near, second, last]


def plane_order(size, at):
    return [at ^ r if size == 4 else jnp.int32(r) for r in range(size)]


def plane_gather(part, axis, size):
    if size != 4:
        whole = lax.all_gather(part, axis, axis=0)
        return [whole[i] for i in range(size)]
    one = lax.ppermute(part, axis, xor_pairs(4, 1))
    two = lax.ppermute(part, axis, xor_pairs(4, 2))
    half = part.shape[-2] // 2
    first = lax.ppermute(two[..., :half, :], axis, xor_pairs(4, 1))
    other = lax.ppermute(one[..., half:, :], axis, xor_pairs(4, 2))
    return [part, one, two, jnp.concatenate([first, other], axis=-2)]


def pair_order(size, at):
    return [at ^ r if size == 2 else jnp.int32(r) for r in range(size)]


def pair_gather(part, axis, size):
    if size != 2:
        whole = lax.all_gather(part, axis, axis=0)
        return [whole[i] for i in range(size)]
    return [part, lax.ppermute(part, axis, xor_pairs(2, 1))]


def normalize_kernel(order, tokens, gain, out):
    features = tokens[...].astype(F32)
    mean_square = jnp.mean(features * features, axis=-1, keepdims=True)
    scale = lax.rsqrt(mean_square + EPSILON)
    count = order.shape[0]
    width = tokens.shape[1] // count
    for r in range(count):
        source = pl.ds(pl.multiple_of(order[r] * width, width), width)
        out[:, r * width : (r + 1) * width] = (
            tokens[:, source].astype(F32) * scale * gain[:, source]
        ).astype(BF16)


def normalize(tokens, norm_gain, order):
    return pl.pallas_call(
        normalize_kernel,
        out_shape=jax.ShapeDtypeStruct(tokens.shape, BF16),
        in_specs=[
            pl.BlockSpec(memory_space=pltpu.SMEM),
            pl.BlockSpec(memory_space=pltpu.VMEM),
            pl.BlockSpec(memory_space=pltpu.VMEM),
        ],
        out_specs=pl.BlockSpec(memory_space=pltpu.VMEM),
        compiler_params=pltpu.CompilerParams(vmem_limit_bytes=16 << 20),
        name="normalize",
    )(order, tokens, norm_gain.reshape(1, -1))


def attention_kernel(
    sizes, places, biases, copies, targets, *refs
):
    groups, reps, heads, spans, slots = sizes
    total = sum(groups)
    queries = refs[: len(groups)]
    pairs = refs[len(groups) : len(groups) * (1 + reps)]
    out, held, asked, sems = refs[len(groups) * (1 + reps) :]
    waits = []
    at = 0
    for g, size in enumerate(groups):
        waits.append(pltpu.make_async_copy(queries[g], asked.at[:, at : at + size], sems.at[len(waits)]))
        for r in range(reps):
            waits.append(
                pltpu.make_async_copy(
                    pairs[g * reps + r], held.at[r, :, :, at : at + size], sems.at[len(waits)]
                )
            )
        at += size
    for copy in waits:
        copy.start()
    for copy in waits:
        copy.wait()
    flat = held.reshape(reps * heads * 2 * total, BLK, HEAD_DIM)
    wanted = asked.reshape(heads * total, BLK, HEAD_DIM)
    factor = HEAD_DIM ** (-0.5) * math.log2(math.e)
    rows = lax.broadcasted_iota(jnp.int32, (BLK, BLK), 0)
    columns = lax.broadcasted_iota(jnp.int32, (BLK, BLK), 1)

    def one_block(j, carry):
        query = wanted[j]
        index = [places[j, n] for n in range(slots)]
        keys = jnp.concatenate([flat[index[n]] for n in range(slots)], axis=0)
        scores = lax.dot_general(
            query, keys, (((1,), (1,)), ((), ())), preferred_element_type=F32
        )
        parts = []
        for n in range(slots):
            part = scores[:, n * BLK : (n + 1) * BLK] * factor
            parts.append(jnp.where(columns <= rows, part, MASKED) if n == 0 else part + biases[j, n])
        top = parts[0]
        for n in range(1, slots):
            top = jnp.maximum(top, parts[n])
        top = jnp.max(top, axis=1, keepdims=True)
        weights = [jnp.exp2(part - top) for part in parts]
        weights[0] = weights[0] * copies[j]
        below = weights[0]
        for n in range(1, slots):
            below = below + weights[n]
        below = jnp.sum(below, axis=1, keepdims=True)
        values = jnp.concatenate([flat[index[n] + total] for n in range(slots)], axis=0)
        blended = jnp.dot(
            jnp.concatenate([w.astype(BF16) for w in weights], axis=1), values, preferred_element_type=F32
        )
        out[targets[j]] = (blended / below).astype(BF16)
        return carry

    lax.fori_loop(0, heads * total, one_block, 0)


def attention(queries, pairs, places, biases, copies, targets, sizes):
    groups, reps, heads, spans, slots = sizes
    total = sum(groups)
    smem = pl.BlockSpec(memory_space=pltpu.SMEM)
    hbm = pl.BlockSpec(memory_space=pl.ANY)
    blocks = heads * total
    return pl.pallas_call(
        functools.partial(attention_kernel, sizes),
        out_shape=jax.ShapeDtypeStruct((blocks, BLK, HEAD_DIM), BF16),
        in_specs=[smem] * 4 + [hbm] * (len(queries) + len(pairs)),
        out_specs=pl.BlockSpec(memory_space=pltpu.VMEM),
        scratch_shapes=[
            pltpu.VMEM((reps, heads, 2, total, BLK, HEAD_DIM), BF16),
            pltpu.VMEM((heads, total, BLK, HEAD_DIM), BF16),
            pltpu.SemaphoreType.DMA((len(groups) * (1 + reps),)),
        ],
        compiler_params=pltpu.CompilerParams(vmem_limit_bytes=40 << 20),
        name="attention",
    )(places, biases, copies, targets, *queries, *pairs)


def shards(heads, reps, lines, tokens, norm_gain, qkv_weight, out_weight, layout):
    head_at, rep_at, line_at = (lax.axis_index(a) for a in ("head", "rep", "line"))
    rows = tokens.shape[0]
    assert rows == BLK
    width = qkv_weight.shape[2]
    spans = heads * reps
    order = jnp.asarray(line_order(lines), jnp.int32)[line_at]
    planes = plane_order(heads, head_at)
    sides = pair_order(reps, rep_at)
    feature_order = jnp.stack([h * reps + r for r in sides for h in planes]).astype(jnp.int32)

    by_plane = plane_gather(qkv_weight, "head", heads)
    by_side = [pair_gather(w, "rep", reps) for w in by_plane]
    weight = jnp.concatenate([by_side[h][r] for r in range(reps) for h in range(heads)], axis=1)

    normed = normalize(tokens, norm_gain, feature_order)
    half = rows // 2
    lower = line_gather(normed[:half], "line", lines)
    upper = line_gather(normed[half:], "line", lines)
    chunks = [jnp.concatenate(pair, axis=0) for pair in zip(lower, upper)]

    groups = (lines - 1, 1)
    queries, pairs = [], []
    at = 0
    for size in groups:
        rows_here = jnp.concatenate(chunks[at : at + size], axis=0)
        at += size
        projected = jnp.einsum("td,cdi->cti", rows_here, weight, preferred_element_type=F32).astype(BF16)
        split = projected.reshape(3, size, BLK, heads, HEAD_DIM).transpose(3, 0, 1, 2, 4)
        mine = lax.all_to_all(split, "head", 0, 0, tiled=True)
        queries.append(mine[:, 0])
        pairs += pair_gather(mine[:, 1:], "rep", reps)

    blocks = spans * lines
    names = jnp.arange(blocks, dtype=jnp.int32)
    slot_of = jnp.argmax(order[None, :] == jnp.arange(lines, dtype=jnp.int32)[:, None], axis=1).astype(jnp.int32)
    span_of = names // lines
    rep_of, head_of = span_of % reps, span_of // reps
    side_of = rep_of ^ rep_at if reps == 2 else rep_of
    place_of = ((side_of * heads + head_of) * 2) * lines + slot_of[names % lines]
    own = (
        (jnp.arange(heads, dtype=jnp.int32)[:, None] * reps + rep_at) * lines + order[None, :]
    ).reshape(-1)
    listed = layout[own]
    before = own - 1
    others = jnp.concatenate([before[:, None], listed], axis=1)
    index = jnp.concatenate([own[:, None], others], axis=1)
    places = place_of[jnp.maximum(index, 0)]
    off = (others < 0) | (others == own[:, None])
    biases = jnp.concatenate([jnp.zeros((own.shape[0], 1), F32), jnp.where(off, MASKED, 0.0)], axis=1)
    copies = 1.0 + jnp.sum(others == own[:, None], axis=1).astype(F32)
    targets = (jnp.arange(heads, dtype=jnp.int32)[:, None] * lines + order[None, :]).reshape(-1)
    attended = attention(
        queries, pairs, places, biases, copies, targets, (groups, reps, heads, spans, index.shape[1])
    )
    landed = lax.all_to_all(attended, ("head", "line"), 0, 0, tiled=True)
    landed = landed.reshape(heads, lines, BLK, HEAD_DIM)[:, order]
    landed = landed.transpose(2, 1, 0, 3).reshape(BLK, lines * heads * HEAD_DIM)
    everyone = jnp.concatenate(pair_gather(landed, "rep", reps), axis=0)

    by_line = line_gather(out_weight, "line", lines)
    projection = jnp.concatenate(
        [jnp.concatenate(plane_gather(w, "head", heads), axis=1) for w in by_line], axis=0
    )
    product = jnp.dot(everyone, projection, preferred_element_type=F32).astype(BF16)
    product = product.reshape(reps, BLK, heads, -1)
    if reps == 2:
        sides_out = [product[0], lax.ppermute(product[1], "rep", xor_pairs(2, 1))]
        columns = [jnp.where(rep_at == k, sides_out[0], sides_out[1]) for k in range(2)]
        columns = jnp.stack(columns, axis=2)
    else:
        columns = lax.all_to_all(product, "rep", 0, 0).transpose(1, 2, 0, 3)
    columns = columns[:, jnp.stack(planes)]
    return columns.reshape(BLK, -1)


def solution(mesh):
    spans, lines = mesh.shape["ctx"], mesh.shape["fsdp"]

    def run(tokens, norm_gain, qkv_weight, out_weight, layout):
        heads = qkv_weight.shape[2] // lines // HEAD_DIM
        reps = spans // heads
        fine = Mesh(mesh.devices.reshape(heads, reps, lines), ("head", "rep", "line"))
        ctx = ("head", "rep")
        rows = P(("head", "rep", "line"), None)
        placed = (rows, P(), P(None, ctx, "line"), P("line", ctx), P())
        return jax.shard_map(
            functools.partial(shards, heads, reps, lines),
            mesh=fine,
            in_specs=placed,
            out_specs=rows,
            check_vma=False,
        )(tokens, norm_gain, qkv_weight, out_weight, layout)

    return run
```

```python
import functools
import math

import jax
import jax.numpy as jnp
import numpy as np
from jax import lax
from jax.experimental import pallas as pl
from jax.experimental.pallas import tpu as pltpu
from jax.sharding import Mesh
from jax.sharding import PartitionSpec as P

HEAD_DIM = 128
BLK = 128
EPSILON = 1e-05
MASKED = -1e30
F32 = jnp.float32
BF16 = jnp.bfloat16


def xor_pairs(size, bit):
    return [(i, i ^ bit) for i in range(size)]


def tie(value, *others):
    return lax.optimization_barrier((value, *others))[0]


def line_order(size):
    if size != 4:
        return [list(range(size))] * size
    return [[0, 1, 2, 3], [1, 0, 2, 3], [2, 3, 1, 0], [3, 2, 1, 0]]


def plane_order(size, at):
    return [at ^ r if size == 4 else jnp.int32(r) for r in range(size)]


def gathered(part, axis, size):
    whole = lax.all_gather(part, axis, axis=0)
    return [whole[i] for i in range(size)]


def pair_gather(part, size):
    if size != 2:
        return gathered(part, "rep", size)
    return [part, lax.ppermute(part, "rep", xor_pairs(2, 1))]


def hop(part, bit):
    return lax.ppermute(part, "head", xor_pairs(4, bit))


def normalize_kernel(order, tokens, gain, out):
    features = tokens[...].astype(F32)
    mean_square = jnp.mean(features * features, axis=-1, keepdims=True)
    scale = lax.rsqrt(mean_square + EPSILON)
    count = order.shape[0]
    width = tokens.shape[1] // count
    for r in range(count):
        source = pl.ds(pl.multiple_of(order[r] * width, width), width)
        out[:, r * width : (r + 1) * width] = (
            tokens[:, source].astype(F32) * scale * gain[:, source]
        ).astype(BF16)


def normalize(tokens, norm_gain, order):
    vmem = pl.BlockSpec(memory_space=pltpu.VMEM)
    return pl.pallas_call(
        normalize_kernel,
        out_shape=jax.ShapeDtypeStruct(tokens.shape, BF16),
        in_specs=[pl.BlockSpec(memory_space=pltpu.SMEM), vmem, vmem],
        out_specs=vmem,
        compiler_params=pltpu.CompilerParams(vmem_limit_bytes=16 << 20),
        name="normalize",
    )(order, tokens, norm_gain.reshape(1, -1))


def attention_kernel(
    sizes, places, biases, copies, targets, *refs
):
    groups, reps, heads, spans, slots = sizes
    total = sum(groups)
    parts = refs[: len(groups) * reps]
    out, held, asked, scores, sems = refs[len(groups) * reps :]
    waits = []
    at = 0
    for g, size in enumerate(groups):
        for r in range(reps):
            ref = parts[g * reps + r]
            to = held.at[r, :, :, at : at + size]
            waits.append(pltpu.make_async_copy(ref.at[:, 1:], to, sems.at[len(waits)]))
        own = parts[g * reps]
        waits.append(pltpu.make_async_copy(own.at[:, 0], asked.at[:, at : at + size], sems.at[len(waits)]))
        at += size
    for copy in waits:
        copy.start()
    for copy in waits:
        copy.wait()
    flat = held.reshape(reps * heads * 2 * total, BLK, HEAD_DIM)
    wanted = asked.reshape(heads * total, BLK, HEAD_DIM)
    blocks = heads * total
    factor = HEAD_DIM ** (-0.5) * math.log2(math.e)
    rows = lax.broadcasted_iota(jnp.int32, (BLK, BLK), 0)
    columns = lax.broadcasted_iota(jnp.int32, (BLK, BLK), 1)

    def score(j, place):
        keys = jnp.concatenate([flat[places[j, n]] for n in range(slots)], axis=0)
        scores[place] = lax.dot_general(wanted[j], keys, (((1,), (1,)), ((), ())), preferred_element_type=F32)

    def blend(j, place):
        parts = []
        for n in range(slots):
            part = scores[place, :, n * BLK : (n + 1) * BLK] * factor
            parts.append(jnp.where(columns <= rows, part, MASKED) if n == 0 else part + biases[j, n])
        top = parts[0]
        for n in range(1, slots):
            top = jnp.maximum(top, parts[n])
        top = jnp.max(top, axis=1, keepdims=True)
        weights = [jnp.exp2(part - top) for part in parts]
        weights[0] = weights[0] * copies[j]
        below = weights[0]
        for n in range(1, slots):
            below = below + weights[n]
        below = jnp.sum(below, axis=1, keepdims=True)
        values = jnp.concatenate([flat[places[j, n] + total] for n in range(slots)], axis=0)
        blended = jnp.dot(
            jnp.concatenate([w.astype(BF16) for w in weights], axis=1), values, preferred_element_type=F32
        )
        out[targets[j]] = (blended / below).astype(BF16)

    score(0, 0)

    def two_blocks(t, carry):
        for place in range(2):
            j = 2 * t + place
            score(jnp.minimum(j + 1, blocks - 1), 1 - place)
            blend(j, place)
        return carry

    lax.fori_loop(0, blocks // 2, two_blocks, 0)


def attention(parts, places, biases, copies, targets, sizes):
    groups, reps, heads, spans, slots = sizes
    total = sum(groups)
    smem = pl.BlockSpec(memory_space=pltpu.SMEM)
    hbm = pl.BlockSpec(memory_space=pl.ANY)
    blocks = heads * total
    return pl.pallas_call(
        functools.partial(attention_kernel, sizes),
        out_shape=jax.ShapeDtypeStruct((blocks, BLK, HEAD_DIM), BF16),
        in_specs=[smem] * 4 + [hbm] * len(parts),
        out_specs=pl.BlockSpec(memory_space=pltpu.VMEM),
        scratch_shapes=[
            pltpu.VMEM((reps, heads, 2, total, BLK, HEAD_DIM), BF16),
            pltpu.VMEM((heads, total, BLK, HEAD_DIM), BF16),
            pltpu.VMEM((2, BLK, slots * BLK), F32),
            pltpu.SemaphoreType.DMA((len(groups) * (1 + reps),)),
        ],
        compiler_params=pltpu.CompilerParams(vmem_limit_bytes=40 << 20),
        cost_estimate=pl.CostEstimate(
            flops=4 * blocks * slots * BLK * BLK * HEAD_DIM,
            bytes_accessed=8 * blocks * BLK * HEAD_DIM * reps,
            transcendentals=blocks * slots * BLK * BLK,
        ),
        name="attention",
    )(places, biases, copies, targets, *parts)


def project_kernel(spots, heads, lines, reps, planes, order, *refs):
    landed, pieces = refs[:reps], refs[reps : reps + len(spots)]
    out, weights, rows, sems = refs[reps + len(spots) :]
    copies = [
        pltpu.make_async_copy(ref, weights.at[s, r, pl.ds(first, ref.shape[0])], sems.at[i])
        for i, ((s, r, first), ref) in enumerate(zip(spots, pieces))
    ]
    for copy in copies:
        copy.start()
    depth = heads * HEAD_DIM
    for k in range(reps):
        for s in range(lines):
            for h in range(heads):
                at = s * depth + h * HEAD_DIM
                rows[k * BLK : (k + 1) * BLK, at : at + HEAD_DIM] = landed[k][h * lines + order[s]]
    width = weights.shape[3]
    for r in range(heads):
        total = None
        for s in range(lines):
            for copy, spot in zip(copies, spots):
                if spot[:2] == (s, r):
                    copy.wait()
            term = jnp.dot(rows[:, s * depth : (s + 1) * depth], weights[s, r], preferred_element_type=F32)
            total = term if total is None else total + term
        place = pl.ds(pl.multiple_of(planes[r] * width, width), width)
        for k in range(reps):
            out[k, :, place] = total[k * BLK : (k + 1) * BLK].astype(BF16)


def project(planes, order, landed, pieces, heads, lines):
    reps = len(landed)
    spots = [piece[:3] for piece in pieces]
    arrays = [piece[3] for piece in pieces]
    width = arrays[0].shape[1]
    depth = heads * HEAD_DIM
    smem = pl.BlockSpec(memory_space=pltpu.SMEM)
    vmem = pl.BlockSpec(memory_space=pltpu.VMEM)
    hbm = pl.BlockSpec(memory_space=pl.ANY)
    return pl.pallas_call(
        functools.partial(project_kernel, spots, heads, lines, reps),
        out_shape=jax.ShapeDtypeStruct((reps, BLK, heads * width), BF16),
        in_specs=[smem] * 2 + [vmem] * reps + [hbm] * len(arrays),
        out_specs=vmem,
        scratch_shapes=[
            pltpu.VMEM((lines, heads, depth, width), BF16),
            pltpu.VMEM((reps * BLK, lines * depth), BF16),
            pltpu.SemaphoreType.DMA((len(arrays),)),
        ],
        compiler_params=pltpu.CompilerParams(vmem_limit_bytes=58 << 20),
        name="project",
    )(planes, order, *landed, *arrays)


def enter_kernel(heads, count, *refs):
    chunks = refs[:count]
    pieces = refs[count:-4]
    out, weights, rows, sems = refs[-4:]
    copies = []
    for c in range(3):
        at = 0
        for piece in pieces:
            target = weights.at[c, pl.ds(at, piece.shape[1])]
            copies.append(pltpu.make_async_copy(piece.at[c], target, sems.at[len(copies)]))
            at += piece.shape[1]
    for copy in copies:
        copy.start()
    for n, chunk in enumerate(chunks):
        rows[n * BLK : (n + 1) * BLK] = chunk[...]
    for c in range(3):
        for copy in copies[c * len(pieces) : (c + 1) * len(pieces)]:
            copy.wait()
        total = jnp.dot(rows[...], weights[c], preferred_element_type=F32).astype(BF16)
        for n in range(count):
            for h in range(heads):
                out[h, c, n] = total[n * BLK : (n + 1) * BLK, h * HEAD_DIM : (h + 1) * HEAD_DIM]


def enter(chunks, pieces, heads):
    features = chunks[0].shape[1]
    vmem = pl.BlockSpec(memory_space=pltpu.VMEM)
    return pl.pallas_call(
        functools.partial(enter_kernel, heads, len(chunks)),
        out_shape=jax.ShapeDtypeStruct((heads, 3, len(chunks), BLK, HEAD_DIM), BF16),
        in_specs=[vmem] * len(chunks) + [pl.BlockSpec(memory_space=pl.ANY)] * len(pieces),
        out_specs=vmem,
        scratch_shapes=[
            pltpu.VMEM((3, features, heads * HEAD_DIM), BF16),
            pltpu.VMEM((len(chunks) * BLK, features), BF16),
            pltpu.SemaphoreType.DMA((3 * len(pieces),)),
        ],
        compiler_params=pltpu.CompilerParams(vmem_limit_bytes=58 << 20),
        cost_estimate=pl.CostEstimate(flops=1, bytes_accessed=1, transcendentals=0),
        name="enter",
    )(*chunks, *pieces)


def leave_kernel(heads, lines, count, order, *refs):
    landed, pieces = refs[:2], refs[2 : 2 + count]
    outs = refs[2 + count : 4 + count]
    weights, rows, sems = refs[4 + count :]
    depth = heads * HEAD_DIM
    width = weights.shape[3]
    copies = []
    for side in range(2):
        for i, (core, first) in enumerate(((0, side), (1, side), (0, 2 + side), (1, 2 + side))):
            at = 0
            for piece in pieces[core::2]:
                source = piece.at[:, pl.ds(first * width, width)]
                target = weights.at[side, i, pl.ds(at, piece.shape[0])]
                copies.append(pltpu.make_async_copy(source, target, sems.at[len(copies)]))
                at += piece.shape[0]
    for copy in copies:
        copy.start()
    for side in range(2):
        for s in range(lines):
            for h in range(heads):
                at = s * depth + h * HEAD_DIM
                rows[side, :, at : at + HEAD_DIM] = landed[side][h * lines + order[s]]
    for side in range(2):
        for i in range(4):
            for copy in copies[(side * 4 + i) * (count // 2) : (side * 4 + i + 1) * (count // 2)]:
                copy.wait()
            outs[side][:, i * width : (i + 1) * width] = jnp.dot(
                rows[side], weights[side, i], preferred_element_type=F32
            ).astype(BF16)


def leave(order, landed_x, landed_y, shared, heads, lines):
    depth = sum(piece.shape[0] for piece in shared[::2])
    width = shared[0].shape[1] // 4
    smem = pl.BlockSpec(memory_space=pltpu.SMEM)
    vmem = pl.BlockSpec(memory_space=pltpu.VMEM)
    hbm = pl.BlockSpec(memory_space=pl.ANY)
    out = jax.ShapeDtypeStruct((BLK, 4 * width), BF16)
    return pl.pallas_call(
        functools.partial(leave_kernel, heads, lines, len(shared)),
        out_shape=(out, out),
        in_specs=[smem] + [vmem] * 2 + [hbm] * len(shared),
        out_specs=(vmem, vmem),
        scratch_shapes=[
            pltpu.VMEM((2, 4, depth, width), BF16),
            pltpu.VMEM((2, BLK, depth), BF16),
            pltpu.SemaphoreType.DMA((4 * len(shared),)),
        ],
        compiler_params=pltpu.CompilerParams(vmem_limit_bytes=58 << 20),
        cost_estimate=pl.CostEstimate(
            flops=16 * BLK * depth * width, bytes_accessed=16 * depth * width, transcendentals=0
        ),
        name="leave",
    )(order, landed_x, landed_y, *shared)


def place_kernel(shifts, own_x, own_y, from_x, from_y, out):
    width = own_x.shape[1] // 4
    for ref, chips, half in ((own_x, (0, 2), 0), (own_y, (0, 1), 1), (from_x, (1, 3), 0), (from_y, (2, 3), 1)):
        for i, chip in enumerate(chips):
            for core in range(2):
                spot = ((shifts[0] ^ chip) * 2 + (shifts[1] ^ core)) * 2 + half
                at = (2 * i + core) * width
                out[:, pl.ds(pl.multiple_of(spot * width, width), width)] = ref[:, at : at + width]


def place(shifts, *parts):
    smem = pl.BlockSpec(memory_space=pltpu.SMEM)
    vmem = pl.BlockSpec(memory_space=pltpu.VMEM)
    return pl.pallas_call(
        place_kernel,
        out_shape=jax.ShapeDtypeStruct((BLK, 4 * parts[0].shape[1]), BF16),
        in_specs=[smem] + [vmem] * 4,
        out_specs=vmem,
        compiler_params=pltpu.CompilerParams(vmem_limit_bytes=16 << 20),
        name="place",
    )(shifts, *parts)


def by_head(projected):
    return lax.all_to_all(projected, "head", 0, 0, tiled=True)


def tables(heads, reps, lines, rep_at, order, layout):
    blocks = heads * reps * lines
    names = jnp.arange(blocks, dtype=jnp.int32)
    slot_of = jnp.argmax(order[None, :] == jnp.arange(lines, dtype=jnp.int32)[:, None], axis=1).astype(jnp.int32)
    span_of = names // lines
    rep_of, head_of = span_of % reps, span_of // reps
    side_of = rep_of ^ rep_at if reps == 2 else rep_of
    place_of = ((side_of * heads + head_of) * 2) * lines + slot_of[names % lines]
    own = ((jnp.arange(heads, dtype=jnp.int32)[:, None] * reps + rep_at) * lines + order[None, :]).reshape(-1)
    others = jnp.concatenate([(own - 1)[:, None], layout[own]], axis=1)
    index = jnp.concatenate([own[:, None], others], axis=1)
    places = place_of[jnp.maximum(index, 0)]
    off = (others < 0) | (others == own[:, None])
    biases = jnp.concatenate([jnp.zeros((own.shape[0], 1), F32), jnp.where(off, MASKED, 0.0)], axis=1)
    copies = 1.0 + jnp.sum(others == own[:, None], axis=1).astype(F32)
    targets = (jnp.arange(heads, dtype=jnp.int32)[:, None] * lines + order[None, :]).reshape(-1)
    return places, biases, copies, targets


def shards(heads, reps, lines, tokens, norm_gain, qkv_weight, out_weight, layout):
    head_at, rep_at, line_at = (lax.axis_index(a) for a in ("head", "rep", "line"))
    assert tokens.shape[0] == BLK
    order = jnp.asarray(line_order(lines), jnp.int32)[line_at]
    planes = plane_order(heads, head_at)
    fast = (heads, reps, lines) == (4, 2, 4)
    feature_order = jnp.stack(
        [(head_at ^ h) * reps + (rep_at ^ r) if fast else jnp.int32(h * reps + r) for r in range(reps) for h in range(heads)]
    ).astype(jnp.int32)
    planes = jnp.stack(planes).astype(jnp.int32)
    if fast:
        w_one, w_two = hop(qkv_weight, 1), hop(qkv_weight, 2)
    normed = normalize(tokens, norm_gain, feature_order)
    table = tables(heads, reps, lines, rep_at, order, layout)
    slots = table[0].shape[1]

    def attend(parts, groups):
        attended = attention(parts, *table, (groups, reps, heads, heads * reps, slots))
        return lax.all_to_all(attended, ("head", "line"), 0, 0, tiled=True)

    if not fast:
        weight = lax.all_gather(qkv_weight, ("head", "rep"), axis=1, tiled=True)
        rows = gathered(normed, "line", lines)
        landed = attend(pair_gather(by_head(enter(rows, [weight], heads)), reps), (lines,))
        out_pieces = [
            (s, h, 0, piece)
            for s, part in enumerate(gathered(out_weight, "line", lines))
            for h, piece in enumerate(gathered(part, "head", heads))
        ]
        product = project(planes, order, pair_gather(landed, reps), out_pieces, heads, lines)
        columns = lax.all_to_all(product, "rep", 0, 0).reshape(reps, BLK, heads, -1)
        return columns.transpose(1, 2, 0, 3).reshape(BLK, -1)

    barrier = lax.optimization_barrier
    inside = (line_at == 1) | (line_at == 2)
    middle, outward, inward = [(1, 2), (2, 1)], [(1, 0), (2, 3)], [(0, 1), (3, 2)]

    def along(part, pairs):
        return lax.ppermute(part, "line", pairs)

    def pair(part):
        return lax.ppermute(part, "rep", xor_pairs(2, 1))

    def share(part):
        width = part.shape[1] // 2
        return hop(part[:, :width], 2), hop(part[:, width:], 1)

    def joined(part, halves):
        return jnp.concatenate([part, *halves], axis=1)

    near, across = along(normed, xor_pairs(4, 1)), along(normed, middle)
    w_pairs = [pair(qkv_weight)]
    near, across, w_pairs[0], *table = barrier((near, across, w_pairs[0], *table))
    crossed, second = along(near, middle), along(across, outward)
    o_in = along(tie(out_weight, near), inward)
    half = w_one.shape[1] // 2
    onward = (w_two[:, :half], w_one[:, half:])
    crossed, second, o_in, w_one, w_two, *onward = barrier((crossed, second, o_in, w_one, w_two, *onward))
    third = along(crossed, outward)
    w_first, w_other = hop(onward[0], 1), hop(onward[1], 2)
    w_pairs += [pair(w) for w in (w_one, w_two)]
    chunk = jnp.where(inside, across, second)
    w_first, w_other, w_pairs[1], w_pairs[2], chunk = barrier((w_first, w_other, w_pairs[1], w_pairs[2], chunk))
    w_pairs += [pair(w) for w in (w_first, w_other)]
    o_own = tie(out_weight, w_first)
    o_out = [along(o_own, outward)]
    o_across = along(o_own, middle)
    first_halves = share(o_own)
    weights = [qkv_weight, w_one, w_two, w_first, w_other, *w_pairs]
    early = enter([normed, near, chunk], weights, heads)
    early, third, o_across, *first_halves = barrier((early, third, o_across, *first_halves))
    o_crossed = along(o_in, middle)
    o_out.append(along(o_across, outward))
    early_heads = by_head(early)
    late = enter([jnp.where(inside, crossed, third)], weights, heads)
    early_heads, late, o_out[0], o_crossed = barrier((early_heads, late, o_out[0], o_crossed))
    near_slot = jnp.where(inside, o_in, o_out[0])
    near_halves = share(near_slot)
    o_out.append(along(o_crossed, outward))
    early_parts = pair_gather(early_heads, reps)
    late_parts = pair_gather(by_head(late), reps)
    early_parts[1], late_parts[1], o_out[1], *near_halves = barrier(
        (early_parts[1], late_parts[1], o_out[1], *near_halves)
    )
    shared = [joined(o_own, first_halves), joined(near_slot, near_halves)]
    attended = attention(early_parts + late_parts, *table, ((lines - 1, 1), reps, heads, heads * reps, slots))
    second_slot = jnp.where(inside, o_across, o_out[1])
    second_halves = share(second_slot)
    attended, o_out[2], *second_halves = barrier((attended, o_out[2], *second_halves))
    landed = lax.all_to_all(attended, ("head", "line"), 0, 0, tiled=True)
    shared.append(joined(second_slot, second_halves))
    third_slot = jnp.where(inside, o_crossed, o_out[2])
    others = [pair(batch) for batch in shared]
    landed, *others = barrier((landed, *others))
    landed_x, landed_y = hop(landed, 1), hop(landed, 2)
    third_halves = share(third_slot)
    shared.append(joined(third_slot, third_halves))
    others.append(pair(shared[3]))
    landed, landed_x, landed_y, others[3] = barrier((landed, landed_x, landed_y, others[3]))
    shared = [batch for both in zip(shared, others) for batch in both]
    shifts = jnp.stack([head_at, rep_at]).astype(jnp.int32)
    to_x, to_y = leave(order, landed_x, landed_y, shared, heads, lines)
    own_x, own_y = leave(order, landed, landed, shared, heads, lines)
    return place(shifts, own_x, own_y, hop(to_x, 1), hop(to_y, 2))


def solution(mesh):
    spans, lines = mesh.shape["ctx"], mesh.shape["fsdp"]

    def run(tokens, norm_gain, qkv_weight, out_weight, layout):
        heads = qkv_weight.shape[2] // lines // HEAD_DIM
        reps = spans // heads
        fine = Mesh(mesh.devices.reshape(heads, reps, lines), ("head", "rep", "line"))
        ctx = ("head", "rep")
        rows = P(("head", "rep", "line"), None)
        placed = (rows, P(), P(None, ctx, "line"), P("line", ctx), P())
        return jax.shard_map(
            functools.partial(shards, heads, reps, lines),
            mesh=fine,
            in_specs=placed,
            out_specs=rows,
            check_vma=False,
        )(tokens, norm_gain, qkv_weight, out_weight, layout)

    return run
```

```python
import functools
import math

import jax
import jax.numpy as jnp
import numpy as np
from jax import lax
from jax.experimental import pallas as pl
from jax.experimental.pallas import tpu as pltpu
from jax.sharding import Mesh
from jax.sharding import PartitionSpec as P

HEAD_DIM = 128
BLK = 128
EPSILON = 1e-05
MASKED = -1e30
F32 = jnp.float32
BF16 = jnp.bfloat16


def xor_pairs(size, bit):
    return [(i, i ^ bit) for i in range(size)]


def tie(value, *others):
    return lax.optimization_barrier((value, *others))[0]


def line_order(size):
    if size != 4:
        return [list(range(size))] * size
    return [[0, 1, 2, 3], [1, 0, 2, 3], [2, 3, 1, 0], [3, 2, 1, 0]]


def plane_order(size, at):
    return [at ^ r if size == 4 else jnp.int32(r) for r in range(size)]


def gathered(part, axis, size):
    whole = lax.all_gather(part, axis, axis=0)
    return [whole[i] for i in range(size)]


def pair_gather(part, size):
    if size != 2:
        return gathered(part, "rep", size)
    return [part, lax.ppermute(part, "rep", xor_pairs(2, 1))]


def hop(part, bit):
    return lax.ppermute(part, "head", xor_pairs(4, bit))


def normalize_kernel(order, tokens, gain, out):
    features = tokens[...].astype(F32)
    mean_square = jnp.mean(features * features, axis=-1, keepdims=True)
    scale = lax.rsqrt(mean_square + EPSILON)
    count = order.shape[0]
    width = tokens.shape[1] // count
    for r in range(count):
        source = pl.ds(pl.multiple_of(order[r] * width, width), width)
        out[:, r * width : (r + 1) * width] = (
            tokens[:, source].astype(F32) * scale * gain[:, source]
        ).astype(BF16)


def normalize(tokens, norm_gain, order):
    vmem = pl.BlockSpec(memory_space=pltpu.VMEM)
    return pl.pallas_call(
        normalize_kernel,
        out_shape=jax.ShapeDtypeStruct(tokens.shape, BF16),
        in_specs=[pl.BlockSpec(memory_space=pltpu.SMEM), vmem, vmem],
        out_specs=vmem,
        compiler_params=pltpu.CompilerParams(vmem_limit_bytes=16 << 20),
        name="normalize",
    )(order, tokens, norm_gain.reshape(1, -1))


def attention_kernel(
    sizes, places, biases, copies, targets, *refs
):
    groups, reps, heads, spans, slots = sizes
    total = sum(groups)
    parts = refs[: len(groups) * reps]
    out, held, asked, scores, sems = refs[len(groups) * reps :]
    waits = []
    at = 0
    for g, size in enumerate(groups):
        for r in range(reps):
            ref = parts[g * reps + r]
            to = held.at[r, :, :, at : at + size]
            waits.append(pltpu.make_async_copy(ref.at[:, 1:], to, sems.at[len(waits)]))
        own = parts[g * reps]
        waits.append(pltpu.make_async_copy(own.at[:, 0], asked.at[:, at : at + size], sems.at[len(waits)]))
        at += size
    for copy in waits:
        copy.start()
    for copy in waits:
        copy.wait()
    flat = held.reshape(reps * heads * 2 * total, BLK, HEAD_DIM)
    wanted = asked.reshape(heads * total, BLK, HEAD_DIM)
    blocks = heads * total
    factor = HEAD_DIM ** (-0.5) * math.log2(math.e)
    rows = lax.broadcasted_iota(jnp.int32, (BLK, BLK), 0)
    columns = lax.broadcasted_iota(jnp.int32, (BLK, BLK), 1)

    def score(j, place):
        keys = jnp.concatenate([flat[places[j, n]] for n in range(slots)], axis=0)
        scores[place] = lax.dot_general(wanted[j], keys, (((1,), (1,)), ((), ())), preferred_element_type=F32)

    def blend(j, place):
        parts = []
        for n in range(slots):
            part = scores[place, :, n * BLK : (n + 1) * BLK] * factor
            parts.append(jnp.where(columns <= rows, part, MASKED) if n == 0 else part + biases[j, n])
        top = parts[0]
        for n in range(1, slots):
            top = jnp.maximum(top, parts[n])
        top = jnp.max(top, axis=1, keepdims=True)
        weights = [jnp.exp2(part - top) for part in parts]
        weights[0] = weights[0] * copies[j]
        below = weights[0]
        for n in range(1, slots):
            below = below + weights[n]
        below = jnp.sum(below, axis=1, keepdims=True)
        values = jnp.concatenate([flat[places[j, n] + total] for n in range(slots)], axis=0)
        blended = jnp.dot(
            jnp.concatenate([w.astype(BF16) for w in weights], axis=1), values, preferred_element_type=F32
        )
        out[targets[j]] = (blended / below).astype(BF16)

    score(0, 0)

    def two_blocks(t, carry):
        for place in range(2):
            j = 2 * t + place
            score(jnp.minimum(j + 1, blocks - 1), 1 - place)
            blend(j, place)
        return carry

    lax.fori_loop(0, blocks // 2, two_blocks, 0)


def attention(parts, places, biases, copies, targets, sizes):
    groups, reps, heads, spans, slots = sizes
    total = sum(groups)
    smem = pl.BlockSpec(memory_space=pltpu.SMEM)
    hbm = pl.BlockSpec(memory_space=pl.ANY)
    blocks = heads * total
    return pl.pallas_call(
        functools.partial(attention_kernel, sizes),
        out_shape=jax.ShapeDtypeStruct((blocks, BLK, HEAD_DIM), BF16),
        in_specs=[smem] * 4 + [hbm] * len(parts),
        out_specs=pl.BlockSpec(memory_space=pltpu.VMEM),
        scratch_shapes=[
            pltpu.VMEM((reps, heads, 2, total, BLK, HEAD_DIM), BF16),
            pltpu.VMEM((heads, total, BLK, HEAD_DIM), BF16),
            pltpu.VMEM((2, BLK, slots * BLK), F32),
            pltpu.SemaphoreType.DMA((len(groups) * (1 + reps),)),
        ],
        compiler_params=pltpu.CompilerParams(vmem_limit_bytes=40 << 20),
        cost_estimate=pl.CostEstimate(
            flops=4 * blocks * slots * BLK * BLK * HEAD_DIM,
            bytes_accessed=8 * blocks * BLK * HEAD_DIM * reps,
            transcendentals=blocks * slots * BLK * BLK,
        ),
        name="attention",
    )(places, biases, copies, targets, *parts)


def project_kernel(spots, heads, lines, reps, planes, order, *refs):
    landed, pieces = refs[:reps], refs[reps : reps + len(spots)]
    out, weights, rows, sems = refs[reps + len(spots) :]
    copies = [
        pltpu.make_async_copy(ref, weights.at[s, r, pl.ds(first, ref.shape[0])], sems.at[i])
        for i, ((s, r, first), ref) in enumerate(zip(spots, pieces))
    ]
    for copy in copies:
        copy.start()
    depth = heads * HEAD_DIM
    for k in range(reps):
        for s in range(lines):
            for h in range(heads):
                at = s * depth + h * HEAD_DIM
                rows[k * BLK : (k + 1) * BLK, at : at + HEAD_DIM] = landed[k][h * lines + order[s]]
    width = weights.shape[3]
    for r in range(heads):
        total = None
        for s in range(lines):
            for copy, spot in zip(copies, spots):
                if spot[:2] == (s, r):
                    copy.wait()
            term = jnp.dot(rows[:, s * depth : (s + 1) * depth], weights[s, r], preferred_element_type=F32)
            total = term if total is None else total + term
        place = pl.ds(pl.multiple_of(planes[r] * width, width), width)
        for k in range(reps):
            out[k, :, place] = total[k * BLK : (k + 1) * BLK].astype(BF16)


def project(planes, order, landed, pieces, heads, lines):
    reps = len(landed)
    spots = [piece[:3] for piece in pieces]
    arrays = [piece[3] for piece in pieces]
    width = arrays[0].shape[1]
    depth = heads * HEAD_DIM
    smem = pl.BlockSpec(memory_space=pltpu.SMEM)
    vmem = pl.BlockSpec(memory_space=pltpu.VMEM)
    hbm = pl.BlockSpec(memory_space=pl.ANY)
    return pl.pallas_call(
        functools.partial(project_kernel, spots, heads, lines, reps),
        out_shape=jax.ShapeDtypeStruct((reps, BLK, heads * width), BF16),
        in_specs=[smem] * 2 + [vmem] * reps + [hbm] * len(arrays),
        out_specs=vmem,
        scratch_shapes=[
            pltpu.VMEM((lines, heads, depth, width), BF16),
            pltpu.VMEM((reps * BLK, lines * depth), BF16),
            pltpu.SemaphoreType.DMA((len(arrays),)),
        ],
        compiler_params=pltpu.CompilerParams(vmem_limit_bytes=58 << 20),
        name="project",
    )(planes, order, *landed, *arrays)


def enter_kernel(heads, chunks, plan, flag, *refs):
    count = sum(chunks)
    rows_in, arrays = refs[:count], refs[count:-5]
    out, weights, rows, row_sems, sems = refs[-5:]
    at = 0
    for n, choices in enumerate(chunks):
        target = rows.at[pl.ds(n * BLK, BLK)]
        if choices == 1:
            pltpu.make_async_copy(rows_in[at], target, row_sems.at[n]).start()
        else:
            for choice in range(2):

                @pl.when(flag[0] == choice)
                def _(choice=choice):
                    pltpu.make_async_copy(rows_in[at + choice], target, row_sems.at[n]).start()

        at += choices
    copies = []
    for c in range(3):
        at = 0
        for i, place in plan[c]:
            size = arrays[i].shape[1]
            target = weights.at[c, pl.ds(at, size)]
            copies.append((c, pltpu.make_async_copy(arrays[i].at[place], target, sems.at[len(copies)])))
            at += size
    for _, copy in copies:
        copy.start()
    at = 0
    for n, choices in enumerate(chunks):
        pltpu.make_async_copy(rows_in[at], rows.at[pl.ds(n * BLK, BLK)], row_sems.at[n]).wait()
        at += choices
    for c in range(3):
        for which, copy in copies:
            if which == c:
                copy.wait()
        total = jnp.dot(rows[...], weights[c], preferred_element_type=F32).astype(BF16)
        for n in range(len(chunks)):
            for h in range(heads):
                out[h, c, n] = total[n * BLK : (n + 1) * BLK, h * HEAD_DIM : (h + 1) * HEAD_DIM]


def enter(flag, chunks, arrays, plan, heads):
    chunks = [chunk if isinstance(chunk, tuple) else (chunk,) for chunk in chunks]
    features = chunks[0][0].shape[1]
    hbm = pl.BlockSpec(memory_space=pl.ANY)
    rows_in = [array for chunk in chunks for array in chunk]
    return pl.pallas_call(
        functools.partial(enter_kernel, heads, [len(chunk) for chunk in chunks], plan),
        out_shape=jax.ShapeDtypeStruct((heads, 3, len(chunks), BLK, HEAD_DIM), BF16),
        in_specs=[pl.BlockSpec(memory_space=pltpu.SMEM)] + [hbm] * (len(rows_in) + len(arrays)),
        out_specs=pl.BlockSpec(memory_space=pltpu.VMEM),
        scratch_shapes=[
            pltpu.VMEM((3, features, heads * HEAD_DIM), BF16),
            pltpu.VMEM((len(chunks) * BLK, features), BF16),
            pltpu.SemaphoreType.DMA((len(chunks),)),
            pltpu.SemaphoreType.DMA((sum(len(parts) for parts in plan),)),
        ],
        compiler_params=pltpu.CompilerParams(vmem_limit_bytes=58 << 20),
        cost_estimate=pl.CostEstimate(flops=1, bytes_accessed=1, transcendentals=0),
        name="enter",
    )(flag, *rows_in, *arrays)


def leave_kernel(heads, lines, count, order, *refs):
    landed, pieces = refs[:2], refs[2 : 2 + 6 * count]
    outs = refs[2 + 6 * count : 4 + 6 * count]
    weights, rows, sems = refs[4 + 6 * count :]
    depth = heads * HEAD_DIM
    width = weights.shape[3]
    copies = []
    for side in range(2):
        for i in range(4):
            at = 0
            for b in range(count):
                batch = pieces[6 * b + 3 * (i % 2) : 6 * b + 3 * (i % 2) + 3]
                source = batch[0].at[:, pl.ds(side * width, width)] if i < 2 else batch[1 + side]
                target = weights.at[side, i, pl.ds(at, source.shape[0])]
                copies.append(pltpu.make_async_copy(source, target, sems.at[len(copies)]))
                at += source.shape[0]
    for copy in copies:
        copy.start()
    for side in range(2):
        for s in range(lines):
            for h in range(heads):
                at = s * depth + h * HEAD_DIM
                rows[side, :, at : at + HEAD_DIM] = landed[side][h * lines + order[s]]
    for side in range(2):
        for i in range(4):
            for copy in copies[(side * 4 + i) * count : (side * 4 + i + 1) * count]:
                copy.wait()
            outs[side][:, i * width : (i + 1) * width] = jnp.dot(
                rows[side], weights[side, i], preferred_element_type=F32
            ).astype(BF16)


def leave(order, landed_x, landed_y, shared, heads, lines):
    depth = sum(batch[0].shape[0] for batch in shared)
    width = shared[0][0].shape[1] // 2
    arrays = [array for batch in shared for array in batch]
    smem = pl.BlockSpec(memory_space=pltpu.SMEM)
    vmem = pl.BlockSpec(memory_space=pltpu.VMEM)
    hbm = pl.BlockSpec(memory_space=pl.ANY)
    out = jax.ShapeDtypeStruct((BLK, 4 * width), BF16)
    return pl.pallas_call(
        functools.partial(leave_kernel, heads, lines, len(shared)),
        out_shape=(out, out),
        in_specs=[smem] + [vmem] * 2 + [hbm] * len(arrays),
        out_specs=(vmem, vmem),
        scratch_shapes=[
            pltpu.VMEM((2, 4, depth, width), BF16),
            pltpu.VMEM((2, BLK, depth), BF16),
            pltpu.SemaphoreType.DMA((8 * len(shared),)),
        ],
        compiler_params=pltpu.CompilerParams(vmem_limit_bytes=58 << 20),
        cost_estimate=pl.CostEstimate(
            flops=16 * BLK * depth * width, bytes_accessed=16 * depth * width, transcendentals=0
        ),
        name="leave",
    )(order, landed_x, landed_y, *arrays)


def place_kernel(shifts, own_x, own_y, from_x, from_y, out):
    width = own_x.shape[1] // 4
    for ref, chips, half in ((own_x, (0, 2), 0), (own_y, (0, 1), 1), (from_x, (1, 3), 0), (from_y, (2, 3), 1)):
        for i, chip in enumerate(chips):
            for core in range(2):
                spot = ((shifts[0] ^ chip) * 2 + (shifts[1] ^ core)) * 2 + half
                at = (2 * i + core) * width
                out[:, pl.ds(pl.multiple_of(spot * width, width), width)] = ref[:, at : at + width]


def place(shifts, *parts):
    smem = pl.BlockSpec(memory_space=pltpu.SMEM)
    vmem = pl.BlockSpec(memory_space=pltpu.VMEM)
    return pl.pallas_call(
        place_kernel,
        out_shape=jax.ShapeDtypeStruct((BLK, 4 * parts[0].shape[1]), BF16),
        in_specs=[smem] + [vmem] * 4,
        out_specs=vmem,
        compiler_params=pltpu.CompilerParams(vmem_limit_bytes=16 << 20),
        name="place",
    )(shifts, *parts)


def by_head(projected):
    return lax.all_to_all(projected, "head", 0, 0, tiled=True)


def tables(heads, reps, lines, rep_at, order, layout):
    blocks = heads * reps * lines
    names = jnp.arange(blocks, dtype=jnp.int32)
    slot_of = jnp.argmax(order[None, :] == jnp.arange(lines, dtype=jnp.int32)[:, None], axis=1).astype(jnp.int32)
    span_of = names // lines
    rep_of, head_of = span_of % reps, span_of // reps
    side_of = rep_of ^ rep_at if reps == 2 else rep_of
    place_of = ((side_of * heads + head_of) * 2) * lines + slot_of[names % lines]
    own = ((jnp.arange(heads, dtype=jnp.int32)[:, None] * reps + rep_at) * lines + order[None, :]).reshape(-1)
    others = jnp.concatenate([(own - 1)[:, None], layout[own]], axis=1)
    index = jnp.concatenate([own[:, None], others], axis=1)
    places = place_of[jnp.maximum(index, 0)]
    off = (others < 0) | (others == own[:, None])
    biases = jnp.concatenate([jnp.zeros((own.shape[0], 1), F32), jnp.where(off, MASKED, 0.0)], axis=1)
    copies = 1.0 + jnp.sum(others == own[:, None], axis=1).astype(F32)
    targets = (jnp.arange(heads, dtype=jnp.int32)[:, None] * lines + order[None, :]).reshape(-1)
    return places, biases, copies, targets


def shards(heads, reps, lines, tokens, norm_gain, qkv_weight, out_weight, layout):
    head_at, rep_at, line_at = (lax.axis_index(a) for a in ("head", "rep", "line"))
    assert tokens.shape[0] == BLK
    order = jnp.asarray(line_order(lines), jnp.int32)[line_at]
    planes = plane_order(heads, head_at)
    fast = (heads, reps, lines) == (4, 2, 4)
    feature_order = jnp.stack(
        [(head_at ^ h) * reps + (rep_at ^ r) if fast else jnp.int32(h * reps + r) for r in range(reps) for h in range(heads)]
    ).astype(jnp.int32)
    planes = jnp.stack(planes).astype(jnp.int32)
    if fast:
        w_one, w_two = hop(qkv_weight, 1), hop(qkv_weight, 2)
    normed = normalize(tokens, norm_gain, feature_order)
    inside = (line_at == 1) | (line_at == 2)
    flag = jnp.where(inside, 0, 1).astype(jnp.int32).reshape(1)
    table = tables(heads, reps, lines, rep_at, order, layout)
    slots = table[0].shape[1]

    def attend(parts, groups):
        attended = attention(parts, *table, (groups, reps, heads, heads * reps, slots))
        return lax.all_to_all(attended, ("head", "line"), 0, 0, tiled=True)

    if not fast:
        weight = lax.all_gather(qkv_weight, ("head", "rep"), axis=1, tiled=True)
        rows = gathered(normed, "line", lines)
        landed = attend(pair_gather(by_head(enter(flag, rows, [weight], [[(0, c)] for c in range(3)], heads)), reps), (lines,))
        out_pieces = [
            (s, h, 0, piece)
            for s, part in enumerate(gathered(out_weight, "line", lines))
            for h, piece in enumerate(gathered(part, "head", heads))
        ]
        product = project(planes, order, pair_gather(landed, reps), out_pieces, heads, lines)
        columns = lax.all_to_all(product, "rep", 0, 0).reshape(reps, BLK, heads, -1)
        return columns.transpose(1, 2, 0, 3).reshape(BLK, -1)

    barrier = lax.optimization_barrier
    middle, outward, inward = [(1, 2), (2, 1)], [(1, 0), (2, 3)], [(0, 1), (3, 2)]

    def along(part, pairs):
        return lax.ppermute(part, "line", pairs)

    def pair(part):
        return lax.ppermute(part, "rep", xor_pairs(2, 1))

    def share(part):
        width = part.shape[1] // 2
        return hop(part[:, :width], 2), hop(part[:, width:], 1)

    near, across = along(normed, xor_pairs(4, 1)), along(normed, middle)
    w_others = [pair(qkv_weight)]
    near, across, w_others[0], *table = barrier((near, across, w_others[0], *table))
    second, crossed = along(across, outward), along(near, middle)
    half = qkv_weight.shape[1] // 2
    w_halves = [w_two[:, :half], w_one[:, half:]]
    o_halves = share(tie(out_weight, w_one, w_two))
    second, crossed, w_one, w_two, *halves = barrier((second, crossed, w_one, w_two, *w_halves, *o_halves))
    w_halves, o_halves = halves[:2], halves[2:]
    third = along(crossed, outward)
    w_first, w_other = hop(w_halves[0], 1), hop(w_halves[1], 2)
    w_others += [pair(w) for w in (w_one, w_two)]
    w_first, w_other, *w_others = barrier((w_first, w_other, *w_others))
    w_others += [pair(w) for w in (w_first, w_other)]
    third, *w_others = barrier((third, *w_others))
    o_own = tie(out_weight, third)
    o_near, o_across = along(o_own, xor_pairs(4, 1)), along(o_own, middle)
    weights = [qkv_weight, w_one, w_two, w_first, w_other, *w_others]
    plan = [[(i, c) for i in range(len(weights))] for c in range(3)]
    chunks = [normed, near, (across, second), (crossed, third)]
    projected, o_near, o_across = barrier((enter(flag, chunks, weights, plan, heads), o_near, o_across))
    mine = by_head(projected)
    o_crossed, o_second = along(o_near, middle), along(o_across, outward)
    mine, o_crossed, o_second = barrier((mine, o_crossed, o_second))
    o_third = along(o_crossed, outward)
    parts = pair_gather(mine, reps)
    batch = jnp.concatenate([o_near, jnp.where(inside, o_across, o_second)], axis=0)
    shared = [[out_weight, *o_halves], [batch, *share(batch)]]
    attended = attention(parts, *table, ((lines,), reps, heads, heads * reps, slots))
    attended, o_third, *shared[1] = barrier((attended, o_third, *shared[1]))
    landed = lax.all_to_all(attended, ("head", "line"), 0, 0, tiled=True)
    last = jnp.where(inside, o_crossed, o_third)
    shared.append([last, *share(last)])
    landed, *others = barrier((landed, *(pair(piece) for pieces in shared for piece in pieces)))
    shared = [pieces + others[3 * i : 3 * i + 3] for i, pieces in enumerate(shared)]
    landed_x, landed_y = hop(landed, 1), hop(landed, 2)
    own_x, own_y = leave(order, landed, landed, shared, heads, lines)
    own_x, own_y, landed_x, landed_y = barrier((own_x, own_y, landed_x, landed_y))
    to_x, to_y = leave(order, landed_x, landed_y, shared, heads, lines)
    shifts = jnp.stack([head_at, rep_at]).astype(jnp.int32)
    return place(shifts, own_x, own_y, hop(to_x, 1), hop(to_y, 2))


def solution(mesh):
    spans, lines = mesh.shape["ctx"], mesh.shape["fsdp"]

    def run(tokens, norm_gain, qkv_weight, out_weight, layout):
        heads = qkv_weight.shape[2] // lines // HEAD_DIM
        reps = spans // heads
        fine = Mesh(mesh.devices.reshape(heads, reps, lines), ("head", "rep", "line"))
        ctx = ("head", "rep")
        rows = P(("head", "rep", "line"), None)
        placed = (rows, P(), P(None, ctx, "line"), P("line", ctx), P())
        return jax.shard_map(
            functools.partial(shards, heads, reps, lines),
            mesh=fine,
            in_specs=placed,
            out_specs=rows,
            check_vma=False,
        )(tokens, norm_gain, qkv_weight, out_weight, layout)

    return run
```

```python
import functools
import math

import jax
import jax.numpy as jnp
import numpy as np
from jax import lax
from jax.experimental import pallas as pl
from jax.experimental.pallas import tpu as pltpu
from jax.sharding import Mesh
from jax.sharding import PartitionSpec as P

HEAD_DIM = 128
BLK = 128
EPSILON = 1e-05
MASKED = -1e30
F32 = jnp.float32
BF16 = jnp.bfloat16


def xor_pairs(size, bit):
    return [(i, i ^ bit) for i in range(size)]


def tie(value, *others):
    return lax.optimization_barrier((value, *others))[0]


def line_order(size):
    if size != 4:
        return [list(range(size))] * size
    return [[0, 1, 2, 3], [1, 0, 2, 3], [2, 3, 1, 0], [3, 2, 1, 0]]


def plane_order(size, at):
    return [at ^ r if size == 4 else jnp.int32(r) for r in range(size)]


def gathered(part, axis, size):
    whole = lax.all_gather(part, axis, axis=0)
    return [whole[i] for i in range(size)]


def pair_gather(part, size):
    if size != 2:
        return gathered(part, "rep", size)
    return [part, lax.ppermute(part, "rep", xor_pairs(2, 1))]


def hop(part, bit):
    return lax.ppermute(part, "head", xor_pairs(4, bit))


def normalize_kernel(order, tokens, gain, out):
    features = tokens[...].astype(F32)
    mean_square = jnp.mean(features * features, axis=-1, keepdims=True)
    scale = lax.rsqrt(mean_square + EPSILON)
    count = order.shape[0]
    width = tokens.shape[1] // count
    for r in range(count):
        source = pl.ds(pl.multiple_of(order[r] * width, width), width)
        out[:, r * width : (r + 1) * width] = (
            tokens[:, source].astype(F32) * scale * gain[:, source]
        ).astype(BF16)


def normalize(tokens, norm_gain, order):
    vmem = pl.BlockSpec(memory_space=pltpu.VMEM)
    return pl.pallas_call(
        normalize_kernel,
        out_shape=jax.ShapeDtypeStruct(tokens.shape, BF16),
        in_specs=[pl.BlockSpec(memory_space=pltpu.SMEM), vmem, vmem],
        out_specs=vmem,
        compiler_params=pltpu.CompilerParams(vmem_limit_bytes=16 << 20),
        name="normalize",
    )(order, tokens, norm_gain.reshape(1, -1))


def attention_kernel(sizes, places, biases, turns, ends, targets, *refs):
    total, reps, heads, buckets = sizes
    parts = refs[:reps]
    out, held, asked, scores, sems = refs[reps:]
    waits = [pltpu.make_async_copy(parts[r].at[:, 1:], held.at[r], sems.at[r]) for r in range(reps)]
    waits.append(pltpu.make_async_copy(parts[0].at[:, 0], asked, sems.at[reps]))
    for copy in waits:
        copy.start()
    for copy in waits:
        copy.wait()
    flat = held.reshape(reps * heads * 2 * total, BLK, HEAD_DIM)
    wanted = asked.reshape(heads * total, BLK, HEAD_DIM)
    factor = HEAD_DIM ** (-0.5) * math.log2(math.e)
    rows = lax.broadcasted_iota(jnp.int32, (BLK, BLK), 0)
    columns = lax.broadcasted_iota(jnp.int32, (BLK, BLK), 1)

    def score(turn, spot, slots):
        j = turns[turn]
        keys = jnp.concatenate([flat[places[j, n]] for n in range(slots)], axis=0)
        scores[spot, :, : slots * BLK] = lax.dot_general(
            wanted[j], keys, (((1,), (1,)), ((), ())), preferred_element_type=F32
        )

    def blend(turn, spot, slots):
        j = turns[turn]
        parts = [scores[spot, :, n * BLK : (n + 1) * BLK] * factor + biases[j, n] for n in range(slots)]
        parts[0] = jnp.where(columns <= rows, parts[0], MASKED)
        top = parts[0]
        for n in range(1, slots):
            top = jnp.maximum(top, parts[n])
        top = jnp.max(top, axis=1, keepdims=True)
        weights = [jnp.exp2(part - top) for part in parts]
        below = weights[0]
        for n in range(1, slots):
            below = below + weights[n]
        below = jnp.sum(below, axis=1, keepdims=True)
        values = jnp.concatenate([flat[places[j, n] + total] for n in range(slots)], axis=0)
        blended = jnp.dot(
            jnp.concatenate([w.astype(BF16) for w in weights], axis=1), values, preferred_element_type=F32
        )
        out[targets[j]] = (blended / below).astype(BF16)

    low = 0
    for b, slots in enumerate(buckets):
        high = ends[b]

        @pl.when(high > low)
        def _(low=low, high=high, slots=slots):
            score(low, 0, slots)

            def two_turns(t, carry):
                turn = low + 2 * t
                score(turn + 1, 1, slots)
                blend(turn, 0, slots)
                score(jnp.minimum(turn + 2, high - 1), 0, slots)
                blend(turn + 1, 1, slots)
                return carry

            pairs = (high - low) // 2
            lax.fori_loop(0, pairs, two_turns, 0)

            @pl.when(low + 2 * pairs < high)
            def _():
                blend(high - 1, 0, slots)

        low = high


def attention(parts, places, biases, turns, ends, targets, buckets):
    heads, _, total = parts[0].shape[:3]
    reps = len(parts)
    smem = pl.BlockSpec(memory_space=pltpu.SMEM)
    blocks, slots = places.shape
    return pl.pallas_call(
        functools.partial(attention_kernel, (total, reps, heads, buckets)),
        out_shape=jax.ShapeDtypeStruct((blocks, BLK, HEAD_DIM), BF16),
        in_specs=[smem] * 5 + [pl.BlockSpec(memory_space=pl.ANY)] * reps,
        out_specs=pl.BlockSpec(memory_space=pltpu.VMEM),
        scratch_shapes=[
            pltpu.VMEM((reps, heads, 2, total, BLK, HEAD_DIM), BF16),
            pltpu.VMEM((heads, total, BLK, HEAD_DIM), BF16),
            pltpu.VMEM((2, BLK, slots * BLK), F32),
            pltpu.SemaphoreType.DMA((reps + 1,)),
        ],
        compiler_params=pltpu.CompilerParams(vmem_limit_bytes=40 << 20),
        cost_estimate=pl.CostEstimate(
            flops=4 * blocks * slots * BLK * BLK * HEAD_DIM,
            bytes_accessed=8 * blocks * BLK * HEAD_DIM * reps,
            transcendentals=blocks * slots * BLK * BLK,
        ),
        name="attention",
    )(places, biases, turns, ends, targets, *parts)


def project_kernel(spots, heads, lines, reps, planes, order, *refs):
    landed, pieces = refs[:reps], refs[reps : reps + len(spots)]
    out, weights, rows, sems = refs[reps + len(spots) :]
    copies = [
        pltpu.make_async_copy(ref, weights.at[s, r, pl.ds(first, ref.shape[0])], sems.at[i])
        for i, ((s, r, first), ref) in enumerate(zip(spots, pieces))
    ]
    for copy in copies:
        copy.start()
    depth = heads * HEAD_DIM
    for k in range(reps):
        for s in range(lines):
            for h in range(heads):
                at = s * depth + h * HEAD_DIM
                rows[k * BLK : (k + 1) * BLK, at : at + HEAD_DIM] = landed[k][h * lines + order[s]]
    width = weights.shape[3]
    for r in range(heads):
        total = None
        for s in range(lines):
            for copy, spot in zip(copies, spots):
                if spot[:2] == (s, r):
                    copy.wait()
            term = jnp.dot(rows[:, s * depth : (s + 1) * depth], weights[s, r], preferred_element_type=F32)
            total = term if total is None else total + term
        place = pl.ds(pl.multiple_of(planes[r] * width, width), width)
        for k in range(reps):
            out[k, :, place] = total[k * BLK : (k + 1) * BLK].astype(BF16)


def project(planes, order, landed, pieces, heads, lines):
    reps = len(landed)
    spots = [piece[:3] for piece in pieces]
    arrays = [piece[3] for piece in pieces]
    width = arrays[0].shape[1]
    depth = heads * HEAD_DIM
    smem = pl.BlockSpec(memory_space=pltpu.SMEM)
    vmem = pl.BlockSpec(memory_space=pltpu.VMEM)
    hbm = pl.BlockSpec(memory_space=pl.ANY)
    return pl.pallas_call(
        functools.partial(project_kernel, spots, heads, lines, reps),
        out_shape=jax.ShapeDtypeStruct((reps, BLK, heads * width), BF16),
        in_specs=[smem] * 2 + [vmem] * reps + [hbm] * len(arrays),
        out_specs=vmem,
        scratch_shapes=[
            pltpu.VMEM((lines, heads, depth, width), BF16),
            pltpu.VMEM((reps * BLK, lines * depth), BF16),
            pltpu.SemaphoreType.DMA((len(arrays),)),
        ],
        compiler_params=pltpu.CompilerParams(vmem_limit_bytes=58 << 20),
        name="project",
    )(planes, order, *landed, *arrays)


def fetch(flag, choices, columns, target, sem):
    copies = [pltpu.make_async_copy(ref.at[:, columns], target, sem) for ref in choices]
    if len(copies) == 1:
        copies[0].start()
    else:
        for choice, copy in enumerate(copies):
            pl.when(flag[0] == choice)(copy.start)
    return copies[0]


def split(refs, counts):
    parts = []
    for count in counts:
        parts.append(refs[:count])
        refs = refs[count:]
    return parts


def fetch_weights(arrays, places, weights, sems):
    copies = []
    for c in range(3):
        row = []
        for i, (ref, place) in enumerate(zip(arrays, places)):
            target = weights.at[c, pl.ds(place, ref.shape[1])]
            row.append(pltpu.make_async_copy(ref.at[c], target, sems.at[c, i]))
            row[-1].start()
        copies.append(row)
    return copies


def begin_kernel(counts, runs, places, flag, *refs):
    chunks = split(refs, counts)
    arrays = refs[sum(counts) : -5]
    out, weights, rows, row_sems, sems = refs[-5:]
    waits = [
        fetch(flag, chunk, pl.ds(0, rows.shape[1]), rows.at[pl.ds(n * BLK, BLK)], row_sems.at[n])
        for n, chunk in enumerate(chunks)
    ]
    copies = fetch_weights(arrays, places, weights, sems)
    for wait in waits:
        wait.wait()
    for c in range(3):
        for copy in copies[c]:
            copy.wait()
        total = None
        at = 0
        for first, size in runs:
            term = jnp.dot(rows[:, first : first + size], weights[c, at : at + size], preferred_element_type=F32)
            total = term if total is None else total + term
            at += size
        out[c] = total


def begin(flag, chunks, arrays, runs):
    chunks = [chunk if isinstance(chunk, tuple) else (chunk,) for chunk in chunks]
    counts = [len(chunk) for chunk in chunks]
    features, width = chunks[0][0].shape[1], arrays[0].shape[2]
    places, at = [], 0
    for array in arrays:
        places.append(at)
        at += array.shape[1]
    hbm = pl.BlockSpec(memory_space=pl.ANY)
    rows_in = [array for chunk in chunks for array in chunk]
    return pl.pallas_call(
        functools.partial(begin_kernel, counts, runs, places),
        out_shape=jax.ShapeDtypeStruct((3, len(chunks) * BLK, width), F32),
        in_specs=[pl.BlockSpec(memory_space=pltpu.SMEM)] + [hbm] * (len(rows_in) + len(arrays)),
        out_specs=pl.BlockSpec(memory_space=pltpu.VMEM),
        scratch_shapes=[
            pltpu.VMEM((3, at, width), BF16),
            pltpu.VMEM((len(chunks) * BLK, features), BF16),
            pltpu.SemaphoreType.DMA((len(chunks),)),
            pltpu.SemaphoreType.DMA((3, len(arrays))),
        ],
        compiler_params=pltpu.CompilerParams(vmem_limit_bytes=58 << 20),
        cost_estimate=pl.CostEstimate(flops=1, bytes_accessed=1, transcendentals=0),
        name="begin",
    )(flag, *rows_in, *arrays)


def enter_kernel(heads, counts, runs, rest, places, flag, begun, *refs):
    chunks = split(refs, counts)
    arrays = refs[sum(counts) : -8]
    out, weights, rows, last, so_far, row_sems, sems, begun_sem = refs[-8:]
    waits = []
    for n, chunk in enumerate(chunks):
        at = 0
        for first, size in runs:
            target = rows.at[pl.ds(n * BLK, BLK), pl.ds(at, size)]
            waits.append(fetch(flag, chunk, pl.ds(first, size), target, row_sems.at[len(waits)]))
            at += size
    common = at
    at = 0
    for first, size in rest:
        waits.append(fetch(flag, chunks[-1], pl.ds(first, size), last.at[:, pl.ds(at, size)], row_sems.at[len(waits)]))
        at += size
    copies = fetch_weights(arrays, places, weights, sems)
    begun_copy = pltpu.make_async_copy(begun, so_far, begun_sem)
    begun_copy.start()
    for wait in waits:
        wait.wait()
    early = so_far.shape[1]
    for c in range(3):
        for copy in copies[c]:
            copy.wait()
        if c == 0:
            begun_copy.wait()
        total = jnp.dot(rows[...], weights[c, :common], preferred_element_type=F32)
        final = total[early:] + jnp.dot(last[...], weights[c, common:], preferred_element_type=F32)
        parts = [(so_far[c] + total[:early]).astype(BF16), final.astype(BF16)]
        for n in range(len(chunks)):
            part, row = (parts[1], 0) if n * BLK == early else (parts[0], n * BLK)
            for h in range(heads):
                out[h, c, n] = part[row : row + BLK, h * HEAD_DIM : (h + 1) * HEAD_DIM]


def enter(flag, begun, chunks, arrays, places, runs, rest, heads):
    chunks = [chunk if isinstance(chunk, tuple) else (chunk,) for chunk in chunks]
    counts = [len(chunk) for chunk in chunks]
    features, width = chunks[0][0].shape[1], arrays[0].shape[2]
    common = sum(size for _, size in runs)
    hbm = pl.BlockSpec(memory_space=pl.ANY)
    rows_in = [array for chunk in chunks for array in chunk]
    return pl.pallas_call(
        functools.partial(enter_kernel, heads, counts, runs, rest, places),
        out_shape=jax.ShapeDtypeStruct((heads, 3, len(chunks), BLK, HEAD_DIM), BF16),
        in_specs=[pl.BlockSpec(memory_space=pltpu.SMEM)] + [hbm] * (1 + len(rows_in) + len(arrays)),
        out_specs=pl.BlockSpec(memory_space=pltpu.VMEM),
        scratch_shapes=[
            pltpu.VMEM((3, features, width), BF16),
            pltpu.VMEM((len(chunks) * BLK, common), BF16),
            pltpu.VMEM((BLK, features - common), BF16),
            pltpu.VMEM(begun.shape, F32),
            pltpu.SemaphoreType.DMA((len(chunks) * len(runs) + len(rest),)),
            pltpu.SemaphoreType.DMA((3, len(arrays))),
            pltpu.SemaphoreType.DMA,
        ],
        compiler_params=pltpu.CompilerParams(vmem_limit_bytes=58 << 20),
        cost_estimate=pl.CostEstimate(flops=1, bytes_accessed=1, transcendentals=0),
        name="enter",
    )(flag, begun, *rows_in, *arrays)


def leave_kernel(heads, lines, count, order, *refs):
    landed, pieces = refs[:2], refs[2 : 2 + 6 * count]
    outs = refs[2 + 6 * count : 4 + 6 * count]
    weights, rows, sems = refs[4 + 6 * count :]
    depth = heads * HEAD_DIM
    width = weights.shape[3]
    copies = []
    for side in range(2):
        for i in range(4):
            at = 0
            for b in range(count):
                batch = pieces[6 * b + 3 * (i % 2) : 6 * b + 3 * (i % 2) + 3]
                source = batch[0].at[:, pl.ds(side * width, width)] if i < 2 else batch[1 + side]
                target = weights.at[side, i, pl.ds(at, source.shape[0])]
                copies.append(pltpu.make_async_copy(source, target, sems.at[len(copies)]))
                at += source.shape[0]
    for copy in copies:
        copy.start()
    for side in range(2):
        for s in range(lines):
            for h in range(heads):
                at = s * depth + h * HEAD_DIM
                rows[side, :, at : at + HEAD_DIM] = landed[side][h * lines + order[s]]
    for side in range(2):
        for i in range(4):
            for copy in copies[(side * 4 + i) * count : (side * 4 + i + 1) * count]:
                copy.wait()
            outs[side][:, i * width : (i + 1) * width] = jnp.dot(
                rows[side], weights[side, i], preferred_element_type=F32
            ).astype(BF16)


def leave(order, landed_x, landed_y, shared, heads, lines):
    depth = sum(batch[0].shape[0] for batch in shared)
    width = shared[0][0].shape[1] // 2
    arrays = [array for batch in shared for array in batch]
    smem = pl.BlockSpec(memory_space=pltpu.SMEM)
    vmem = pl.BlockSpec(memory_space=pltpu.VMEM)
    hbm = pl.BlockSpec(memory_space=pl.ANY)
    out = jax.ShapeDtypeStruct((BLK, 4 * width), BF16)
    return pl.pallas_call(
        functools.partial(leave_kernel, heads, lines, len(shared)),
        out_shape=(out, out),
        in_specs=[smem] + [vmem] * 2 + [hbm] * len(arrays),
        out_specs=(vmem, vmem),
        scratch_shapes=[
            pltpu.VMEM((2, 4, depth, width), BF16),
            pltpu.VMEM((2, BLK, depth), BF16),
            pltpu.SemaphoreType.DMA((8 * len(shared),)),
        ],
        compiler_params=pltpu.CompilerParams(vmem_limit_bytes=58 << 20),
        cost_estimate=pl.CostEstimate(
            flops=16 * BLK * depth * width, bytes_accessed=16 * depth * width, transcendentals=0
        ),
        name="leave",
    )(order, landed_x, landed_y, *arrays)


def place_kernel(shifts, own_x, own_y, from_x, from_y, out):
    width = own_x.shape[1] // 4
    for ref, chips, half in ((own_x, (0, 2), 0), (own_y, (0, 1), 1), (from_x, (1, 3), 0), (from_y, (2, 3), 1)):
        for i, chip in enumerate(chips):
            for core in range(2):
                spot = ((shifts[0] ^ chip) * 2 + (shifts[1] ^ core)) * 2 + half
                at = (2 * i + core) * width
                out[:, pl.ds(pl.multiple_of(spot * width, width), width)] = ref[:, at : at + width]


def place(shifts, *parts):
    smem = pl.BlockSpec(memory_space=pltpu.SMEM)
    vmem = pl.BlockSpec(memory_space=pltpu.VMEM)
    return pl.pallas_call(
        place_kernel,
        out_shape=jax.ShapeDtypeStruct((BLK, 4 * parts[0].shape[1]), BF16),
        in_specs=[smem] + [vmem] * 4,
        out_specs=vmem,
        compiler_params=pltpu.CompilerParams(vmem_limit_bytes=16 << 20),
        name="place",
    )(shifts, *parts)


def by_head(projected):
    return lax.all_to_all(projected, "head", 0, 0, tiled=True)


def tables(heads, reps, lines, rep_at, order, layout, buckets):
    ints = jnp.int32

    def place_of(block):
        span = block // lines
        side = (span % reps) ^ rep_at if reps == 2 else span % reps
        slot = jnp.sum(jnp.where(block[..., None] % lines == order, jnp.arange(lines, dtype=ints), 0), axis=-1)
        return ((side * heads + span // reps) * 2) * lines + slot

    own = ((jnp.arange(heads, dtype=ints)[:, None] * reps + rep_at) * lines + order[None, :]).reshape(-1)
    listed = jnp.sum(
        jnp.where(own[:, None, None] == jnp.arange(layout.shape[0], dtype=ints)[None, :, None], layout[None], 0), axis=1
    )
    others = jnp.concatenate([(own - 1)[:, None], listed], axis=1)
    count = others.shape[1]
    at = jnp.arange(count, dtype=ints)
    mine = others == own[:, None]
    kept = (others >= 0) & ~mine
    same = (others[:, :, None] == others[:, None, :]) & kept[:, None, :]
    often = jnp.sum(same, axis=2)
    first = kept & ~jnp.any(same & (at[None, :] < at[:, None])[None], axis=2)
    rank = jnp.sum(first[:, None, :] & (at[None, :] < at[:, None])[None], axis=2)
    chosen = first[:, None, :] & (rank[:, None, :] == at[None, :, None])
    block = jnp.sum(jnp.where(chosen, others[:, None, :], 0), axis=2)
    times = jnp.sum(jnp.where(chosen, often[:, None, :], 0), axis=2)
    places = place_of(jnp.concatenate([own[:, None], jnp.where(times > 0, block, own[:, None])], axis=1))
    times = jnp.concatenate([1 + jnp.sum(mine, axis=1, keepdims=True), times], axis=1)
    biases = jnp.where(times > 0, jnp.log2(jnp.maximum(times, 1).astype(F32)), MASKED)
    distinct = jnp.sum(times > 0, axis=1)
    bucket = sum((distinct > size).astype(ints) for size in buckets[:-1])
    here = jnp.arange(own.shape[0], dtype=ints)
    ahead = (bucket[None, :] < bucket[:, None]) | ((bucket[None, :] == bucket[:, None]) & (here[None, :] < here[:, None]))
    turn = jnp.sum(ahead, axis=1)
    turns = jnp.sum(jnp.where(turn[None, :] == here[:, None], here[None, :], 0), axis=1)
    ends = jnp.sum(bucket[None, :] <= jnp.arange(len(buckets), dtype=ints)[:, None], axis=1)
    targets = (jnp.arange(heads, dtype=ints)[:, None] * lines + order[None, :]).reshape(-1)
    return places.astype(ints), biases, turns.astype(ints), ends.astype(ints), targets


def shards(heads, reps, lines, tokens, norm_gain, qkv_weight, out_weight, layout):
    head_at, rep_at, line_at = (lax.axis_index(a) for a in ("head", "rep", "line"))
    assert tokens.shape[0] == BLK
    order = jnp.asarray(line_order(lines), jnp.int32)[line_at]
    planes = plane_order(heads, head_at)
    fast = (heads, reps, lines) == (4, 2, 4)
    feature_order = jnp.stack(
        [(head_at ^ h) * reps + (rep_at ^ r) if fast else jnp.int32(h * reps + r) for r in range(reps) for h in range(heads)]
    ).astype(jnp.int32)
    planes = jnp.stack(planes).astype(jnp.int32)
    if fast:
        w_one, w_two = hop(qkv_weight, 1), hop(qkv_weight, 2)
    normed = normalize(tokens, norm_gain, feature_order)
    inside = (line_at == 1) | (line_at == 2)
    flag = jnp.where(inside, 0, 1).astype(jnp.int32).reshape(1)
    slots = 2 + layout.shape[1]
    buckets = sorted({min(8, slots), min(12, slots), slots})
    table = tables(heads, reps, lines, rep_at, order, layout, buckets)

    if not fast:
        weight = lax.all_gather(qkv_weight, ("head", "rep"), axis=1, tiled=True)
        rows = gathered(normed, "line", lines)
        whole = begin(flag, rows, [weight], [(0, weight.shape[1])]).astype(BF16)
        projected = whole.reshape(3, lines, BLK, heads, HEAD_DIM).transpose(3, 0, 1, 2, 4)
        attended = attention(pair_gather(by_head(projected), reps), *table, buckets)
        landed = lax.all_to_all(attended, ("head", "line"), 0, 0, tiled=True)
        out_pieces = [
            (s, h, 0, piece)
            for s, part in enumerate(gathered(out_weight, "line", lines))
            for h, piece in enumerate(gathered(part, "head", heads))
        ]
        product = project(planes, order, pair_gather(landed, reps), out_pieces, heads, lines)
        columns = lax.all_to_all(product, "rep", 0, 0).reshape(reps, BLK, heads, -1)
        return columns.transpose(1, 2, 0, 3).reshape(BLK, -1)

    barrier = lax.optimization_barrier
    middle, outward, inward = [(1, 2), (2, 1)], [(1, 0), (2, 3)], [(0, 1), (3, 2)]

    def along(part, pairs):
        return lax.ppermute(part, "line", pairs)

    def pair(part):
        return lax.ppermute(part, "rep", xor_pairs(2, 1))

    def share(part):
        width = part.shape[1] // 2
        return hop(part[:, :width], 2), hop(part[:, width:], 1)

    near, across = along(normed, xor_pairs(4, 1)), along(normed, middle)
    w_others = [pair(qkv_weight)]
    near, across, w_others[0], *table = barrier((near, across, w_others[0], *table))
    second, crossed = along(across, outward), along(near, middle)
    half = qkv_weight.shape[1] // 2
    w_halves = [w_two[:, :half], w_one[:, half:]]
    o_halves = share(tie(out_weight, w_one, w_two))
    second, crossed, w_one, w_two, *halves = barrier((second, crossed, w_one, w_two, *w_halves, *o_halves))
    w_halves, o_halves = halves[:2], halves[2:]
    third = along(crossed, outward)
    w_first, w_other = hop(w_halves[0], 1), hop(w_halves[1], 2)
    w_others += [pair(w) for w in (w_one, w_two)]
    size = qkv_weight.shape[1]
    near_runs, far_runs = [(0, 3 * size), (4 * size, 3 * size)], [(3 * size, size), (7 * size, size)]
    chunks = [normed, near, (across, second)]
    near_weights = [qkv_weight, w_one, w_two, *w_others]
    begun = begin(flag, chunks, near_weights, near_runs)
    w_first, w_other, begun = barrier((w_first, w_other, begun))
    w_others = [pair(w) for w in (w_first, w_other)]
    third, o_own, *w_others = barrier((third, out_weight, *w_others))
    chunks.append((crossed, third))
    o_near, o_across = along(o_own, xor_pairs(4, 1)), along(o_own, middle)
    weights = [w_first, w_other, *w_others, *near_weights]
    places = [0, half, 2 * half, 3 * half] + [2 * size + i * size for i in range(6)]
    projected = enter(flag, begun, chunks, weights, places, far_runs, near_runs, heads)
    projected, o_near, o_across = barrier((projected, o_near, o_across))
    mine = by_head(projected)
    o_crossed, o_second = along(o_near, middle), along(o_across, outward)
    mine, o_crossed, o_second = barrier((mine, o_crossed, o_second))
    o_third = along(o_crossed, outward)
    parts = pair_gather(mine, reps)
    batch = jnp.concatenate([o_near, jnp.where(inside, o_across, o_second)], axis=0)
    shared = [[out_weight, *o_halves], [batch, *share(batch)]]
    attended = attention(parts, *table, buckets)
    attended, o_third, *shared[1] = barrier((attended, o_third, *shared[1]))
    landed = lax.all_to_all(attended, ("head", "line"), 0, 0, tiled=True)
    last = jnp.where(inside, o_crossed, o_third)
    shared.append([last, *share(last)])
    landed, *others = barrier((landed, *(pair(piece) for pieces in shared for piece in pieces)))
    shared = [pieces + others[3 * i : 3 * i + 3] for i, pieces in enumerate(shared)]
    landed_x, landed_y = hop(landed, 1), hop(landed, 2)
    own_x, own_y = leave(order, landed, landed, shared, heads, lines)
    own_x, own_y, landed_x, landed_y = barrier((own_x, own_y, landed_x, landed_y))
    to_x, to_y = leave(order, landed_x, landed_y, shared, heads, lines)
    shifts = jnp.stack([head_at, rep_at]).astype(jnp.int32)
    return place(shifts, own_x, own_y, hop(to_x, 1), hop(to_y, 2))


def solution(mesh):
    spans, lines = mesh.shape["ctx"], mesh.shape["fsdp"]

    def run(tokens, norm_gain, qkv_weight, out_weight, layout):
        heads = qkv_weight.shape[2] // lines // HEAD_DIM
        reps = spans // heads
        fine = Mesh(mesh.devices.reshape(heads, reps, lines), ("head", "rep", "line"))
        ctx = ("head", "rep")
        rows = P(("head", "rep", "line"), None)
        placed = (rows, P(), P(None, ctx, "line"), P("line", ctx), P())
        return jax.shard_map(
            functools.partial(shards, heads, reps, lines),
            mesh=fine,
            in_specs=placed,
            out_specs=rows,
            check_vma=False,
        )(tokens, norm_gain, qkv_weight, out_weight, layout)

    return run
```

```python
import functools
import math

import jax
import jax.numpy as jnp
import numpy as np
from jax import lax
from jax.experimental import pallas as pl
from jax.experimental.pallas import tpu as pltpu
from jax.sharding import Mesh
from jax.sharding import PartitionSpec as P

HEAD_DIM = 128
BLK = 128
EPSILON = 1e-05
MASKED = -1e30
F32 = jnp.float32
BF16 = jnp.bfloat16


def xor_pairs(size, bit):
    return [(i, i ^ bit) for i in range(size)]


def tie(value, *others):
    return lax.optimization_barrier((value, *others))[0]


def line_order(size):
    if size != 4:
        return [list(range(size))] * size
    return [[0, 1, 2, 3], [1, 0, 2, 3], [2, 3, 1, 0], [3, 2, 1, 0]]


def plane_order(size, at):
    return [at ^ r if size == 4 else jnp.int32(r) for r in range(size)]


def gathered(part, axis, size):
    whole = lax.all_gather(part, axis, axis=0)
    return [whole[i] for i in range(size)]


def pair_gather(part, size):
    if size != 2:
        return gathered(part, "rep", size)
    return [part, lax.ppermute(part, "rep", xor_pairs(2, 1))]


def hop(part, bit):
    return lax.ppermute(part, "head", xor_pairs(4, bit))


def normalize_rows(rows, order, gain):
    width = rows.shape[1] // order.shape[0]
    parts = [slice(r * width, (r + 1) * width) for r in range(order.shape[0])]
    total = None
    for part in parts:
        features = rows[:, part].astype(F32)
        squares = jnp.sum(features * features, axis=-1, keepdims=True)
        total = squares if total is None else total + squares
    scale = lax.rsqrt(total * (1.0 / rows.shape[1]) + EPSILON)
    for r, part in enumerate(parts):
        place = pl.ds(pl.multiple_of(order[r] * width, width), width)
        rows[:, part] = (rows[:, part].astype(F32) * scale * gain[:, place]).astype(BF16)


def normalize_kernel(order, tokens, gain, out):
    out[...] = tokens[...]
    normalize_rows(out, order, gain)


def normalize(tokens, norm_gain, order):
    vmem = pl.BlockSpec(memory_space=pltpu.VMEM)
    return pl.pallas_call(
        normalize_kernel,
        out_shape=jax.ShapeDtypeStruct(tokens.shape, BF16),
        in_specs=[pl.BlockSpec(memory_space=pltpu.SMEM), vmem, vmem],
        out_specs=vmem,
        compiler_params=pltpu.CompilerParams(vmem_limit_bytes=16 << 20),
        name="normalize",
    )(order, tokens, norm_gain)


def attention_kernel(sizes, places, biases, turns, ends, targets, *refs):
    total, reps, heads, buckets = sizes
    parts = refs[:reps]
    out, held, asked, scores, sems = refs[reps:]
    waits = [pltpu.make_async_copy(parts[r].at[:, 1:], held.at[r], sems.at[r]) for r in range(reps)]
    waits.append(pltpu.make_async_copy(parts[0].at[:, 0], asked, sems.at[reps]))
    for copy in waits:
        copy.start()
    for copy in waits:
        copy.wait()
    flat = held.reshape(reps * heads * 2 * total, BLK, HEAD_DIM)
    wanted = asked.reshape(heads * total, BLK, HEAD_DIM)
    factor = HEAD_DIM ** (-0.5) * math.log2(math.e)
    rows = lax.broadcasted_iota(jnp.int32, (BLK, BLK), 0)
    columns = lax.broadcasted_iota(jnp.int32, (BLK, BLK), 1)

    def score(turn, spot, slots):
        j = turns[turn]
        keys = jnp.concatenate([flat[places[j, n]] for n in range(slots)], axis=0)
        scores[spot, :, : slots * BLK] = lax.dot_general(
            wanted[j], keys, (((1,), (1,)), ((), ())), preferred_element_type=F32
        )

    def blend(turn, spot, slots):
        j = turns[turn]
        parts = [scores[spot, :, n * BLK : (n + 1) * BLK] * factor + biases[j, n] for n in range(slots)]
        parts[0] = jnp.where(columns <= rows, parts[0], MASKED)
        top = parts[0]
        for n in range(1, slots):
            top = jnp.maximum(top, parts[n])
        top = jnp.max(top, axis=1, keepdims=True)
        weights = [jnp.exp2(part - top) for part in parts]
        below = weights[0]
        for n in range(1, slots):
            below = below + weights[n]
        below = jnp.sum(below, axis=1, keepdims=True)
        values = jnp.concatenate([flat[places[j, n] + total] for n in range(slots)], axis=0)
        blended = jnp.dot(
            jnp.concatenate([w.astype(BF16) for w in weights], axis=1), values, preferred_element_type=F32
        )
        out[targets[j]] = (blended / below).astype(BF16)

    low = 0
    for b, slots in enumerate(buckets):
        high = ends[b]

        @pl.when(high > low)
        def _(low=low, high=high, slots=slots):
            score(low, 0, slots)

            def two_turns(t, carry):
                turn = low + 2 * t
                score(turn + 1, 1, slots)
                blend(turn, 0, slots)
                score(jnp.minimum(turn + 2, high - 1), 0, slots)
                blend(turn + 1, 1, slots)
                return carry

            pairs = (high - low) // 2
            lax.fori_loop(0, pairs, two_turns, 0)

            @pl.when(low + 2 * pairs < high)
            def _():
                blend(high - 1, 0, slots)

        low = high


def attention(parts, places, biases, turns, ends, targets, buckets):
    heads, _, total = parts[0].shape[:3]
    reps = len(parts)
    smem = pl.BlockSpec(memory_space=pltpu.SMEM)
    blocks, slots = places.shape
    return pl.pallas_call(
        functools.partial(attention_kernel, (total, reps, heads, buckets)),
        out_shape=jax.ShapeDtypeStruct((blocks, BLK, HEAD_DIM), BF16),
        in_specs=[smem] * 5 + [pl.BlockSpec(memory_space=pl.ANY)] * reps,
        out_specs=pl.BlockSpec(memory_space=pltpu.VMEM),
        scratch_shapes=[
            pltpu.VMEM((reps, heads, 2, total, BLK, HEAD_DIM), BF16),
            pltpu.VMEM((heads, total, BLK, HEAD_DIM), BF16),
            pltpu.VMEM((2, BLK, slots * BLK), F32),
            pltpu.SemaphoreType.DMA((reps + 1,)),
        ],
        compiler_params=pltpu.CompilerParams(vmem_limit_bytes=40 << 20),
        cost_estimate=pl.CostEstimate(
            flops=4 * blocks * slots * BLK * BLK * HEAD_DIM,
            bytes_accessed=8 * blocks * BLK * HEAD_DIM * reps,
            transcendentals=blocks * slots * BLK * BLK,
        ),
        name="attention",
    )(places, biases, turns, ends, targets, *parts)


def project_kernel(spots, heads, lines, reps, planes, order, *refs):
    landed, pieces = refs[:reps], refs[reps : reps + len(spots)]
    out, weights, rows, sems = refs[reps + len(spots) :]
    copies = [
        pltpu.make_async_copy(ref, weights.at[s, r, pl.ds(first, ref.shape[0])], sems.at[i])
        for i, ((s, r, first), ref) in enumerate(zip(spots, pieces))
    ]
    for copy in copies:
        copy.start()
    depth = heads * HEAD_DIM
    for k in range(reps):
        for s in range(lines):
            for h in range(heads):
                at = s * depth + h * HEAD_DIM
                rows[k * BLK : (k + 1) * BLK, at : at + HEAD_DIM] = landed[k][h * lines + order[s]]
    width = weights.shape[3]
    for r in range(heads):
        total = None
        for s in range(lines):
            for copy, spot in zip(copies, spots):
                if spot[:2] == (s, r):
                    copy.wait()
            term = jnp.dot(rows[:, s * depth : (s + 1) * depth], weights[s, r], preferred_element_type=F32)
            total = term if total is None else total + term
        place = pl.ds(pl.multiple_of(planes[r] * width, width), width)
        for k in range(reps):
            out[k, :, place] = total[k * BLK : (k + 1) * BLK].astype(BF16)


def project(planes, order, landed, pieces, heads, lines):
    reps = len(landed)
    spots = [piece[:3] for piece in pieces]
    arrays = [piece[3] for piece in pieces]
    width = arrays[0].shape[1]
    depth = heads * HEAD_DIM
    smem = pl.BlockSpec(memory_space=pltpu.SMEM)
    vmem = pl.BlockSpec(memory_space=pltpu.VMEM)
    hbm = pl.BlockSpec(memory_space=pl.ANY)
    return pl.pallas_call(
        functools.partial(project_kernel, spots, heads, lines, reps),
        out_shape=jax.ShapeDtypeStruct((reps, BLK, heads * width), BF16),
        in_specs=[smem] * 2 + [vmem] * reps + [hbm] * len(arrays),
        out_specs=vmem,
        scratch_shapes=[
            pltpu.VMEM((lines, heads, depth, width), BF16),
            pltpu.VMEM((reps * BLK, lines * depth), BF16),
            pltpu.SemaphoreType.DMA((len(arrays),)),
        ],
        compiler_params=pltpu.CompilerParams(vmem_limit_bytes=58 << 20),
        name="project",
    )(planes, order, *landed, *arrays)


def fetch(flag, order, choices, target, sem):
    count = order.shape[0]
    width = target.shape[1] // count

    def start(ref):
        for r in range(count):
            source = ref.at[:, pl.ds(pl.multiple_of(order[r] * width, width), width)]
            pltpu.make_async_copy(source, target.at[:, pl.ds(r * width, width)], sem).start()

    if len(choices) == 1:
        start(choices[0])
    else:
        for choice, ref in enumerate(choices):
            pl.when(flag[0] == choice)(functools.partial(start, ref))
    return pltpu.make_async_copy(choices[0], target, sem)


def split(refs, counts):
    parts = []
    for count in counts:
        parts.append(refs[:count])
        refs = refs[count:]
    return parts


def fetch_weights(arrays, places, weights, sems):
    copies = []
    for c in range(3):
        row = []
        for i, (ref, place) in enumerate(zip(arrays, places)):
            target = weights.at[c, pl.ds(place, ref.shape[1])]
            row.append(pltpu.make_async_copy(ref.at[c], target, sems.at[c, i]))
            row[-1].start()
        copies.append(row)
    return copies


def begin_kernel(counts, runs, rest, places, raw, flag, order, gain, *refs):
    chunks = split(refs, counts)
    arrays = refs[sum(counts) : -6]
    out, left, weights, rows, row_sems, sems = refs[-6:]
    waits = []
    for n, chunk in enumerate(chunks):
        target = rows.at[pl.ds(n * BLK, BLK)]
        if raw:
            waits.append(fetch(flag, order, chunk, target, row_sems.at[n]))
        else:
            waits.append(pltpu.make_async_copy(chunk[0], target, row_sems.at[n]))
            waits[-1].start()
    copies = fetch_weights(arrays, places, weights, sems)
    for wait in waits:
        wait.wait()
    if raw:
        normalize_rows(rows, order, gain)
    at = 0
    for first, size in rest:
        left[:, at : at + size] = rows[:, first : first + size]
        at += size
    for c in range(3):
        for copy in copies[c]:
            copy.wait()
        total = None
        at = 0
        for first, size in runs:
            term = jnp.dot(rows[:, first : first + size], weights[c, at : at + size], preferred_element_type=F32)
            total = term if total is None else total + term
            at += size
        out[c] = total


def begin(flag, order, gain, chunks, arrays, runs, rest, raw):
    chunks = [chunk if isinstance(chunk, tuple) else (chunk,) for chunk in chunks]
    counts = [len(chunk) for chunk in chunks]
    features, width = chunks[0][0].shape[1], arrays[0].shape[2]
    rows = len(chunks) * BLK
    places, at = [], 0
    for array in arrays:
        places.append(at)
        at += array.shape[1]
    smem = pl.BlockSpec(memory_space=pltpu.SMEM)
    vmem = pl.BlockSpec(memory_space=pltpu.VMEM)
    hbm = pl.BlockSpec(memory_space=pl.ANY)
    rows_in = [array for chunk in chunks for array in chunk]
    return pl.pallas_call(
        functools.partial(begin_kernel, counts, runs, rest, places, raw),
        out_shape=(
            jax.ShapeDtypeStruct((3, rows, width), F32),
            jax.ShapeDtypeStruct((rows, max(HEAD_DIM, sum(size for _, size in rest))), BF16),
        ),
        in_specs=[smem, smem, vmem] + [hbm] * (len(rows_in) + len(arrays)),
        out_specs=(vmem, vmem),
        scratch_shapes=[
            pltpu.VMEM((3, at, width), BF16),
            pltpu.VMEM((rows, features), BF16),
            pltpu.SemaphoreType.DMA((len(chunks),)),
            pltpu.SemaphoreType.DMA((3, len(arrays))),
        ],
        compiler_params=pltpu.CompilerParams(vmem_limit_bytes=58 << 20),
        cost_estimate=pl.CostEstimate(flops=1, bytes_accessed=1, transcendentals=0),
        name="begin",
    )(flag, order, gain, *rows_in, *arrays)


def enter_kernel(heads, runs, rest, places, flag, order, gain, begun, left, *refs):
    chunk, arrays = refs[:2], refs[2:-7]
    out, weights, rows, last, so_far, other_sems, sems = refs[-7:]
    early = so_far.shape[1]
    last_copy = fetch(flag, order, chunk, last, other_sems.at[0])
    left_copy = pltpu.make_async_copy(left, rows.at[pl.ds(0, early)], other_sems.at[1])
    begun_copy = pltpu.make_async_copy(begun, so_far, other_sems.at[2])
    left_copy.start()
    copies = fetch_weights(arrays, places, weights, sems)
    begun_copy.start()
    last_copy.wait()
    normalize_rows(last, order, gain)
    at = 0
    for first, size in runs:
        rows[early:, at : at + size] = last[:, first : first + size]
        at += size
    common = at
    left_copy.wait()
    for c in range(3):
        for copy in copies[c]:
            copy.wait()
        if c == 0:
            begun_copy.wait()
        total = jnp.dot(rows[...], weights[c, :common], preferred_element_type=F32)
        final = total[early:]
        at = common
        for first, size in rest:
            final = final + jnp.dot(
                last[:, first : first + size], weights[c, at : at + size], preferred_element_type=F32
            )
            at += size
        parts = [(so_far[c] + total[:early]).astype(BF16), final.astype(BF16)]
        for n in range(early // BLK + 1):
            part, row = (parts[1], 0) if n * BLK == early else (parts[0], n * BLK)
            for h in range(heads):
                out[h, c, n] = part[row : row + BLK, h * HEAD_DIM : (h + 1) * HEAD_DIM]


def enter(flag, order, gain, begun, left, chunk, arrays, places, runs, rest, heads):
    features, width = chunk[0].shape[1], arrays[0].shape[2]
    early, common = left.shape
    smem = pl.BlockSpec(memory_space=pltpu.SMEM)
    vmem = pl.BlockSpec(memory_space=pltpu.VMEM)
    hbm = pl.BlockSpec(memory_space=pl.ANY)
    return pl.pallas_call(
        functools.partial(enter_kernel, heads, runs, rest, places),
        out_shape=jax.ShapeDtypeStruct((heads, 3, early // BLK + 1, BLK, HEAD_DIM), BF16),
        in_specs=[smem, smem, vmem] + [hbm] * (4 + len(arrays)),
        out_specs=vmem,
        scratch_shapes=[
            pltpu.VMEM((3, features, width), BF16),
            pltpu.VMEM((early + BLK, common), BF16),
            pltpu.VMEM((BLK, features), BF16),
            pltpu.VMEM(begun.shape, F32),
            pltpu.SemaphoreType.DMA((3,)),
            pltpu.SemaphoreType.DMA((3, len(arrays))),
        ],
        compiler_params=pltpu.CompilerParams(vmem_limit_bytes=58 << 20),
        cost_estimate=pl.CostEstimate(flops=1, bytes_accessed=1, transcendentals=0),
        name="enter",
    )(flag, order, gain, begun, left, *chunk, *arrays)


def leave_kernel(heads, lines, count, order, *refs):
    landed, pieces = refs[:2], refs[2 : 2 + 6 * count]
    outs = refs[2 + 6 * count : 4 + 6 * count]
    both, beside, rows, sems = refs[4 + 6 * count :]
    depth = heads * HEAD_DIM
    width = beside.shape[3]
    copies = []
    for kind in range(3):
        for core in range(2):
            at = 0
            for b in range(count):
                source = pieces[6 * b + 3 * core + kind]
                target = beside.at[kind - 1, core] if kind else both.at[core]
                copies.append(
                    pltpu.make_async_copy(source, target.at[pl.ds(at, source.shape[0])], sems.at[len(copies)])
                )
                copies[-1].start()
                at += source.shape[0]
    for side in range(2):
        for s in range(lines):
            for h in range(heads):
                at = s * depth + h * HEAD_DIM
                rows[side, :, at : at + HEAD_DIM] = landed[side][h * lines + order[s]]
    for kind in range(3):
        for core in range(2):
            for copy in copies[(kind * 2 + core) * count : (kind * 2 + core + 1) * count]:
                copy.wait()
            for side in range(2) if kind == 0 else (kind - 1,):
                weight = beside[kind - 1, core] if kind else both[core, :, side * width : (side + 1) * width]
                at = (2 * (kind > 0) + core) * width
                outs[side][:, at : at + width] = jnp.dot(
                    rows[side], weight, preferred_element_type=F32
                ).astype(BF16)


def leave(order, landed_x, landed_y, shared, heads, lines):
    depth = sum(batch[0].shape[0] for batch in shared)
    width = shared[0][0].shape[1] // 2
    arrays = [array for batch in shared for array in batch]
    smem = pl.BlockSpec(memory_space=pltpu.SMEM)
    vmem = pl.BlockSpec(memory_space=pltpu.VMEM)
    hbm = pl.BlockSpec(memory_space=pl.ANY)
    out = jax.ShapeDtypeStruct((BLK, 4 * width), BF16)
    return pl.pallas_call(
        functools.partial(leave_kernel, heads, lines, len(shared)),
        out_shape=(out, out),
        in_specs=[smem] + [vmem] * 2 + [hbm] * len(arrays),
        out_specs=(vmem, vmem),
        scratch_shapes=[
            pltpu.VMEM((2, depth, 2 * width), BF16),
            pltpu.VMEM((2, 2, depth, width), BF16),
            pltpu.VMEM((2, BLK, depth), BF16),
            pltpu.SemaphoreType.DMA((6 * len(shared),)),
        ],
        compiler_params=pltpu.CompilerParams(vmem_limit_bytes=58 << 20),
        cost_estimate=pl.CostEstimate(
            flops=16 * BLK * depth * width, bytes_accessed=16 * depth * width, transcendentals=0
        ),
        name="leave",
    )(order, landed_x, landed_y, *arrays)


def place_kernel(shifts, own_x, own_y, from_x, from_y, out):
    width = own_x.shape[1] // 4
    for ref, chips, half in ((own_x, (0, 2), 0), (own_y, (0, 1), 1), (from_x, (1, 3), 0), (from_y, (2, 3), 1)):
        for i, chip in enumerate(chips):
            for core in range(2):
                spot = ((shifts[0] ^ chip) * 2 + (shifts[1] ^ core)) * 2 + half
                at = (2 * i + core) * width
                out[:, pl.ds(pl.multiple_of(spot * width, width), width)] = ref[:, at : at + width]


def place(shifts, *parts):
    smem = pl.BlockSpec(memory_space=pltpu.SMEM)
    vmem = pl.BlockSpec(memory_space=pltpu.VMEM)
    return pl.pallas_call(
        place_kernel,
        out_shape=jax.ShapeDtypeStruct((BLK, 4 * parts[0].shape[1]), BF16),
        in_specs=[smem] + [vmem] * 4,
        out_specs=vmem,
        compiler_params=pltpu.CompilerParams(vmem_limit_bytes=16 << 20),
        name="place",
    )(shifts, *parts)


def by_head(projected):
    return lax.all_to_all(projected, "head", 0, 0, tiled=True)


def tables(heads, reps, lines, rep_at, order, layout, buckets):
    ints = jnp.int32

    def place_of(block):
        span = block // lines
        side = (span % reps) ^ rep_at if reps == 2 else span % reps
        slot = jnp.sum(jnp.where(block[..., None] % lines == order, jnp.arange(lines, dtype=ints), 0), axis=-1)
        return ((side * heads + span // reps) * 2) * lines + slot

    own = ((jnp.arange(heads, dtype=ints)[:, None] * reps + rep_at) * lines + order[None, :]).reshape(-1)
    listed = jnp.sum(
        jnp.where(own[:, None, None] == jnp.arange(layout.shape[0], dtype=ints)[None, :, None], layout[None], 0), axis=1
    )
    others = jnp.concatenate([(own - 1)[:, None], listed], axis=1)
    count = others.shape[1]
    at = jnp.arange(count, dtype=ints)
    mine = others == own[:, None]
    kept = (others >= 0) & ~mine
    same = (others[:, :, None] == others[:, None, :]) & kept[:, None, :]
    often = jnp.sum(same, axis=2)
    first = kept & ~jnp.any(same & (at[None, :] < at[:, None])[None], axis=2)
    rank = jnp.sum(first[:, None, :] & (at[None, :] < at[:, None])[None], axis=2)
    chosen = first[:, None, :] & (rank[:, None, :] == at[None, :, None])
    block = jnp.sum(jnp.where(chosen, others[:, None, :], 0), axis=2)
    times = jnp.sum(jnp.where(chosen, often[:, None, :], 0), axis=2)
    places = place_of(jnp.concatenate([own[:, None], jnp.where(times > 0, block, own[:, None])], axis=1))
    times = jnp.concatenate([1 + jnp.sum(mine, axis=1, keepdims=True), times], axis=1)
    biases = jnp.where(times > 0, jnp.log2(jnp.maximum(times, 1).astype(F32)), MASKED)
    distinct = jnp.sum(times > 0, axis=1)
    bucket = sum((distinct > size).astype(ints) for size in buckets[:-1])
    here = jnp.arange(own.shape[0], dtype=ints)
    ahead = (bucket[None, :] < bucket[:, None]) | ((bucket[None, :] == bucket[:, None]) & (here[None, :] < here[:, None]))
    turn = jnp.sum(ahead, axis=1)
    turns = jnp.sum(jnp.where(turn[None, :] == here[:, None], here[None, :], 0), axis=1)
    ends = jnp.sum(bucket[None, :] <= jnp.arange(len(buckets), dtype=ints)[:, None], axis=1)
    targets = (jnp.arange(heads, dtype=ints)[:, None] * lines + order[None, :]).reshape(-1)
    return places.astype(ints), biases, turns.astype(ints), ends.astype(ints), targets


def shards(heads, reps, lines, tokens, norm_gain, qkv_weight, out_weight, layout):
    head_at, rep_at, line_at = (lax.axis_index(a) for a in ("head", "rep", "line"))
    assert tokens.shape[0] == BLK
    order = jnp.asarray(line_order(lines), jnp.int32)[line_at]
    planes = plane_order(heads, head_at)
    fast = (heads, reps, lines) == (4, 2, 4)
    feature_order = jnp.stack(
        [(head_at ^ h) * reps + (rep_at ^ r) if fast else jnp.int32(h * reps + r) for r in range(reps) for h in range(heads)]
    ).astype(jnp.int32)
    planes = jnp.stack(planes).astype(jnp.int32)
    if fast:
        w_one, w_two = hop(qkv_weight, 1), hop(qkv_weight, 2)
    gain = norm_gain.reshape(1, -1)
    inside = (line_at == 1) | (line_at == 2)
    flag = jnp.where(inside, 0, 1).astype(jnp.int32).reshape(1)
    slots = 2 + layout.shape[1]
    buckets = sorted({min(8, slots), min(12, slots), slots})
    table = tables(heads, reps, lines, rep_at, order, layout, buckets)

    if not fast:
        weight = lax.all_gather(qkv_weight, ("head", "rep"), axis=1, tiled=True)
        rows = gathered(normalize(tokens, gain, feature_order), "line", lines)
        runs = [(0, weight.shape[1])]
        whole, _ = begin(flag, feature_order, gain, rows, [weight], runs, [], False)
        projected = whole.astype(BF16).reshape(3, lines, BLK, heads, HEAD_DIM).transpose(3, 0, 1, 2, 4)
        attended = attention(pair_gather(by_head(projected), reps), *table, buckets)
        landed = lax.all_to_all(attended, ("head", "line"), 0, 0, tiled=True)
        out_pieces = [
            (s, h, 0, piece)
            for s, part in enumerate(gathered(out_weight, "line", lines))
            for h, piece in enumerate(gathered(part, "head", heads))
        ]
        product = project(planes, order, pair_gather(landed, reps), out_pieces, heads, lines)
        columns = lax.all_to_all(product, "rep", 0, 0).reshape(reps, BLK, heads, -1)
        return columns.transpose(1, 2, 0, 3).reshape(BLK, -1)

    barrier = lax.optimization_barrier
    middle, outward, inward = [(1, 2), (2, 1)], [(1, 0), (2, 3)], [(0, 1), (3, 2)]

    def along(part, pairs):
        return lax.ppermute(part, "line", pairs)

    def pair(part):
        return lax.ppermute(part, "rep", xor_pairs(2, 1))

    def share(part):
        width = part.shape[1] // 2
        return hop(part[:, :width], 2), hop(part[:, width:], 1)

    near, across = along(tokens, xor_pairs(4, 1)), along(tokens, middle)
    w_others = [pair(qkv_weight)]
    near, across, w_others[0], *table = barrier((near, across, w_others[0], *table))
    second, crossed = along(across, outward), along(near, middle)
    half = qkv_weight.shape[1] // 2
    w_halves = [w_two[:, :half], w_one[:, half:]]
    o_halves = share(tie(out_weight, w_one, w_two))
    second, crossed, w_one, w_two, *halves = barrier((second, crossed, w_one, w_two, *w_halves, *o_halves))
    w_halves, o_halves = halves[:2], halves[2:]
    third = along(crossed, outward)
    w_first, w_other = hop(w_halves[0], 1), hop(w_halves[1], 2)
    w_others += [pair(w) for w in (w_one, w_two)]
    size = qkv_weight.shape[1]
    near_runs, far_runs = [(0, 3 * size), (4 * size, 3 * size)], [(3 * size, size), (7 * size, size)]
    chunks = [tokens, near, (across, second)]
    near_weights = [qkv_weight, w_one, w_two, *w_others]
    begun, left = begin(flag, feature_order, gain, chunks, near_weights, near_runs, far_runs, True)
    w_first, w_other, begun, left = barrier((w_first, w_other, begun, left))
    w_others = [pair(w) for w in (w_first, w_other)]
    third, o_own, *w_others = barrier((third, out_weight, *w_others))
    o_near, o_across = along(o_own, xor_pairs(4, 1)), along(o_own, middle)
    weights = [w_first, w_other, *w_others, *near_weights]
    places = [0, half, 2 * half, 3 * half] + [2 * size + i * size for i in range(6)]
    projected = enter(
        flag, feature_order, gain, begun, left, (crossed, third), weights, places, far_runs, near_runs, heads
    )
    projected, o_near, o_across = barrier((projected, o_near, o_across))
    mine = by_head(projected)
    o_crossed, o_second = along(o_near, middle), along(o_across, outward)
    mine, o_crossed, o_second = barrier((mine, o_crossed, o_second))
    o_third = along(o_crossed, outward)
    parts = pair_gather(mine, reps)
    batch = jnp.concatenate([o_near, jnp.where(inside, o_across, o_second)], axis=0)
    shared = [[out_weight, *o_halves], [batch, *share(batch)]]
    attended = attention(parts, *table, buckets)
    attended, o_third, *shared[1] = barrier((attended, o_third, *shared[1]))
    landed = lax.all_to_all(attended, ("head", "line"), 0, 0, tiled=True)
    last = jnp.where(inside, o_crossed, o_third)
    shared.append([last, *share(last)])
    landed, *others = barrier((landed, *(pair(piece) for pieces in shared for piece in pieces)))
    shared = [pieces + others[3 * i : 3 * i + 3] for i, pieces in enumerate(shared)]
    landed_x, landed_y = hop(landed, 1), hop(landed, 2)
    own_x, own_y = leave(order, landed, landed, shared, heads, lines)
    own_x, own_y, landed_x, landed_y = barrier((own_x, own_y, landed_x, landed_y))
    to_x, to_y = leave(order, landed_x, landed_y, shared, heads, lines)
    shifts = jnp.stack([head_at, rep_at]).astype(jnp.int32)
    return place(shifts, own_x, own_y, hop(to_x, 1), hop(to_y, 2))


def solution(mesh):
    spans, lines = mesh.shape["ctx"], mesh.shape["fsdp"]

    def run(tokens, norm_gain, qkv_weight, out_weight, layout):
        heads = qkv_weight.shape[2] // lines // HEAD_DIM
        reps = spans // heads
        fine = Mesh(mesh.devices.reshape(heads, reps, lines), ("head", "rep", "line"))
        ctx = ("head", "rep")
        rows = P(("head", "rep", "line"), None)
        placed = (rows, P(), P(None, ctx, "line"), P("line", ctx), P())
        return jax.shard_map(
            functools.partial(shards, heads, reps, lines),
            mesh=fine,
            in_specs=placed,
            out_specs=rows,
            check_vma=False,
        )(tokens, norm_gain, qkv_weight, out_weight, layout)

    return run
```

```python
import functools
import math

import jax
import jax.numpy as jnp
import numpy as np
from jax import lax
from jax.experimental import pallas as pl
from jax.experimental.pallas import tpu as pltpu
from jax.sharding import Mesh
from jax.sharding import PartitionSpec as P

HEAD_DIM = 128
BLK = 128
EPSILON = 1e-05
MASKED = -1e30
F32 = jnp.float32
BF16 = jnp.bfloat16


def xor_pairs(size, bit):
    return [(i, i ^ bit) for i in range(size)]


def tie(value, *others):
    return lax.optimization_barrier((value, *others))[0]


def line_order(size):
    if size != 4:
        return [list(range(size))] * size
    return [[0, 1, 2, 3], [1, 0, 2, 3], [2, 3, 1, 0], [3, 2, 1, 0]]


def plane_order(size, at):
    return [at ^ r if size == 4 else jnp.int32(r) for r in range(size)]


def gathered(part, axis, size):
    whole = lax.all_gather(part, axis, axis=0)
    return [whole[i] for i in range(size)]


def pair_gather(part, size):
    if size != 2:
        return gathered(part, "rep", size)
    return [part, lax.ppermute(part, "rep", xor_pairs(2, 1))]


def hop(part, bit):
    return lax.ppermute(part, "head", xor_pairs(4, bit))


def normalize_rows(rows, order, gain):
    width = rows.shape[1] // order.shape[0]
    parts = [slice(r * width, (r + 1) * width) for r in range(order.shape[0])]
    total = None
    for part in parts:
        features = rows[:, part].astype(F32)
        squares = jnp.sum(features * features, axis=-1, keepdims=True)
        total = squares if total is None else total + squares
    scale = lax.rsqrt(total * (1.0 / rows.shape[1]) + EPSILON)
    for r, part in enumerate(parts):
        place = pl.ds(pl.multiple_of(order[r] * width, width), width)
        rows[:, part] = (rows[:, part].astype(F32) * scale * gain[:, place]).astype(BF16)


def normalize_kernel(order, tokens, gain, out):
    out[...] = tokens[...]
    normalize_rows(out, order, gain)


def normalize(tokens, norm_gain, order):
    vmem = pl.BlockSpec(memory_space=pltpu.VMEM)
    return pl.pallas_call(
        normalize_kernel,
        out_shape=jax.ShapeDtypeStruct(tokens.shape, BF16),
        in_specs=[pl.BlockSpec(memory_space=pltpu.SMEM), vmem, vmem],
        out_specs=vmem,
        compiler_params=pltpu.CompilerParams(vmem_limit_bytes=16 << 20),
        name="normalize",
    )(order, tokens, norm_gain)


def attention_kernel(sizes, places, biases, turns, ends, targets, *refs):
    total, reps, heads, buckets = sizes
    parts = refs[:reps]
    out, held, asked, scores, sems = refs[reps:]
    waits = [pltpu.make_async_copy(parts[r].at[:, 1:], held.at[r], sems.at[r]) for r in range(reps)]
    waits.append(pltpu.make_async_copy(parts[0].at[:, 0], asked, sems.at[reps]))
    for copy in waits:
        copy.start()
    for copy in waits:
        copy.wait()
    flat = held.reshape(reps * heads * 2 * total, BLK, HEAD_DIM)
    wanted = asked.reshape(heads * total, BLK, HEAD_DIM)
    factor = HEAD_DIM ** (-0.5) * math.log2(math.e)
    rows = lax.broadcasted_iota(jnp.int32, (BLK, BLK), 0)
    columns = lax.broadcasted_iota(jnp.int32, (BLK, BLK), 1)

    def score(turn, spot, slots):
        j = turns[turn]
        keys = jnp.concatenate([flat[places[j, n]] for n in range(slots)], axis=0)
        scores[spot, :, : slots * BLK] = lax.dot_general(
            wanted[j], keys, (((1,), (1,)), ((), ())), preferred_element_type=F32
        )

    def blend(turn, spot, slots):
        j = turns[turn]
        parts = [scores[spot, :, n * BLK : (n + 1) * BLK] * factor + biases[j, n] for n in range(slots)]
        parts[0] = jnp.where(columns <= rows, parts[0], MASKED)
        top = parts[0]
        for n in range(1, slots):
            top = jnp.maximum(top, parts[n])
        top = jnp.max(top, axis=1, keepdims=True)
        weights = [jnp.exp2(part - top) for part in parts]
        below = weights[0]
        for n in range(1, slots):
            below = below + weights[n]
        below = jnp.sum(below, axis=1, keepdims=True)
        values = jnp.concatenate([flat[places[j, n] + total] for n in range(slots)], axis=0)
        blended = jnp.dot(
            jnp.concatenate([w.astype(BF16) for w in weights], axis=1), values, preferred_element_type=F32
        )
        out[targets[j]] = (blended / below).astype(BF16)

    low = 0
    for b, slots in enumerate(buckets):
        high = ends[b]

        @pl.when(high > low)
        def _(low=low, high=high, slots=slots):
            score(low, 0, slots)

            def two_turns(t, carry):
                turn = low + 2 * t
                score(turn + 1, 1, slots)
                blend(turn, 0, slots)
                score(jnp.minimum(turn + 2, high - 1), 0, slots)
                blend(turn + 1, 1, slots)
                return carry

            pairs = (high - low) // 2
            lax.fori_loop(0, pairs, two_turns, 0)

            @pl.when(low + 2 * pairs < high)
            def _():
                blend(high - 1, 0, slots)

        low = high


def attention(parts, places, biases, turns, ends, targets, buckets):
    heads, _, total = parts[0].shape[:3]
    reps = len(parts)
    smem = pl.BlockSpec(memory_space=pltpu.SMEM)
    blocks, slots = places.shape
    return pl.pallas_call(
        functools.partial(attention_kernel, (total, reps, heads, buckets)),
        out_shape=jax.ShapeDtypeStruct((blocks, BLK, HEAD_DIM), BF16),
        in_specs=[smem] * 5 + [pl.BlockSpec(memory_space=pl.ANY)] * reps,
        out_specs=pl.BlockSpec(memory_space=pltpu.VMEM),
        scratch_shapes=[
            pltpu.VMEM((reps, heads, 2, total, BLK, HEAD_DIM), BF16),
            pltpu.VMEM((heads, total, BLK, HEAD_DIM), BF16),
            pltpu.VMEM((2, BLK, slots * BLK), F32),
            pltpu.SemaphoreType.DMA((reps + 1,)),
        ],
        compiler_params=pltpu.CompilerParams(vmem_limit_bytes=40 << 20),
        cost_estimate=pl.CostEstimate(
            flops=4 * blocks * slots * BLK * BLK * HEAD_DIM,
            bytes_accessed=8 * blocks * BLK * HEAD_DIM * reps,
            transcendentals=blocks * slots * BLK * BLK,
        ),
        name="attention",
    )(places, biases, turns, ends, targets, *parts)


def project_kernel(spots, heads, lines, reps, planes, order, *refs):
    landed, pieces = refs[:reps], refs[reps : reps + len(spots)]
    out, weights, rows, sems = refs[reps + len(spots) :]
    copies = [
        pltpu.make_async_copy(ref, weights.at[s, r, pl.ds(first, ref.shape[0])], sems.at[i])
        for i, ((s, r, first), ref) in enumerate(zip(spots, pieces))
    ]
    for copy in copies:
        copy.start()
    depth = heads * HEAD_DIM
    for k in range(reps):
        for s in range(lines):
            for h in range(heads):
                at = s * depth + h * HEAD_DIM
                rows[k * BLK : (k + 1) * BLK, at : at + HEAD_DIM] = landed[k][h * lines + order[s]]
    width = weights.shape[3]
    for r in range(heads):
        total = None
        for s in range(lines):
            for copy, spot in zip(copies, spots):
                if spot[:2] == (s, r):
                    copy.wait()
            term = jnp.dot(rows[:, s * depth : (s + 1) * depth], weights[s, r], preferred_element_type=F32)
            total = term if total is None else total + term
        place = pl.ds(pl.multiple_of(planes[r] * width, width), width)
        for k in range(reps):
            out[k, :, place] = total[k * BLK : (k + 1) * BLK].astype(BF16)


def project(planes, order, landed, pieces, heads, lines):
    reps = len(landed)
    spots = [piece[:3] for piece in pieces]
    arrays = [piece[3] for piece in pieces]
    width = arrays[0].shape[1]
    depth = heads * HEAD_DIM
    smem = pl.BlockSpec(memory_space=pltpu.SMEM)
    vmem = pl.BlockSpec(memory_space=pltpu.VMEM)
    hbm = pl.BlockSpec(memory_space=pl.ANY)
    return pl.pallas_call(
        functools.partial(project_kernel, spots, heads, lines, reps),
        out_shape=jax.ShapeDtypeStruct((reps, BLK, heads * width), BF16),
        in_specs=[smem] * 2 + [vmem] * reps + [hbm] * len(arrays),
        out_specs=vmem,
        scratch_shapes=[
            pltpu.VMEM((lines, heads, depth, width), BF16),
            pltpu.VMEM((reps * BLK, lines * depth), BF16),
            pltpu.SemaphoreType.DMA((len(arrays),)),
        ],
        compiler_params=pltpu.CompilerParams(vmem_limit_bytes=58 << 20),
        name="project",
    )(planes, order, *landed, *arrays)


def fetch(flag, order, choices, target, sem):
    count = order.shape[0]
    width = target.shape[1] // count

    def start(ref):
        for r in range(count):
            source = ref.at[:, pl.ds(pl.multiple_of(order[r] * width, width), width)]
            pltpu.make_async_copy(source, target.at[:, pl.ds(r * width, width)], sem).start()

    if len(choices) == 1:
        start(choices[0])
    else:
        for choice, ref in enumerate(choices):
            pl.when(flag[0] == choice)(functools.partial(start, ref))
    return pltpu.make_async_copy(choices[0], target, sem)


def split(refs, counts):
    parts = []
    for count in counts:
        parts.append(refs[:count])
        refs = refs[count:]
    return parts


def fetch_weights(arrays, places, weights, sems):
    copies = []
    for c in range(3):
        row = []
        for i, (ref, place) in enumerate(zip(arrays, places)):
            target = weights.at[c, pl.ds(place, ref.shape[1])]
            row.append(pltpu.make_async_copy(ref.at[c], target, sems.at[c, i]))
            row[-1].start()
        copies.append(row)
    return copies


def begin_kernel(counts, runs, rest, places, raw, flag, order, gain, *refs):
    chunks = split(refs, counts)
    arrays = refs[sum(counts) : -6]
    out, left, weights, rows, row_sems, sems = refs[-6:]
    waits = []
    for n, chunk in enumerate(chunks):
        target = rows.at[pl.ds(n * BLK, BLK)]
        if raw:
            waits.append(fetch(flag, order, chunk, target, row_sems.at[n]))
        else:
            waits.append(pltpu.make_async_copy(chunk[0], target, row_sems.at[n]))
            waits[-1].start()
    copies = fetch_weights(arrays, places, weights, sems)
    for wait in waits:
        wait.wait()
    if raw:
        normalize_rows(rows, order, gain)
    at = 0
    for first, size in rest:
        left[:, at : at + size] = rows[:, first : first + size]
        at += size
    for c in range(3):
        for copy in copies[c]:
            copy.wait()
        total = None
        at = 0
        for first, size in runs:
            term = jnp.dot(rows[:, first : first + size], weights[c, at : at + size], preferred_element_type=F32)
            total = term if total is None else total + term
            at += size
        out[c] = total


def begin(flag, order, gain, chunks, arrays, runs, rest, raw):
    chunks = [chunk if isinstance(chunk, tuple) else (chunk,) for chunk in chunks]
    counts = [len(chunk) for chunk in chunks]
    features, width = chunks[0][0].shape[1], arrays[0].shape[2]
    rows = len(chunks) * BLK
    places, at = [], 0
    for array in arrays:
        places.append(at)
        at += array.shape[1]
    smem = pl.BlockSpec(memory_space=pltpu.SMEM)
    vmem = pl.BlockSpec(memory_space=pltpu.VMEM)
    hbm = pl.BlockSpec(memory_space=pl.ANY)
    rows_in = [array for chunk in chunks for array in chunk]
    return pl.pallas_call(
        functools.partial(begin_kernel, counts, runs, rest, places, raw),
        out_shape=(
            jax.ShapeDtypeStruct((3, rows, width), F32),
            jax.ShapeDtypeStruct((rows, max(HEAD_DIM, sum(size for _, size in rest))), BF16),
        ),
        in_specs=[smem, smem, vmem] + [hbm] * (len(rows_in) + len(arrays)),
        out_specs=(vmem, vmem),
        scratch_shapes=[
            pltpu.VMEM((3, at, width), BF16),
            pltpu.VMEM((rows, features), BF16),
            pltpu.SemaphoreType.DMA((len(chunks),)),
            pltpu.SemaphoreType.DMA((3, len(arrays))),
        ],
        compiler_params=pltpu.CompilerParams(vmem_limit_bytes=58 << 20),
        cost_estimate=pl.CostEstimate(flops=1, bytes_accessed=1, transcendentals=0),
        name="begin",
    )(flag, order, gain, *rows_in, *arrays)


def enter_kernel(heads, runs, rest, places, flag, order, gain, begun, left, *refs):
    chunk, arrays = refs[:2], refs[2:-7]
    out, weights, rows, last, so_far, other_sems, sems = refs[-7:]
    early = so_far.shape[1]
    last_copy = fetch(flag, order, chunk, last, other_sems.at[0])
    left_copy = pltpu.make_async_copy(left, rows.at[pl.ds(0, early)], other_sems.at[1])
    begun_copy = pltpu.make_async_copy(begun, so_far, other_sems.at[2])
    left_copy.start()
    copies = fetch_weights(arrays, places, weights, sems)
    begun_copy.start()
    last_copy.wait()
    normalize_rows(last, order, gain)
    at = 0
    for first, size in runs:
        rows[early:, at : at + size] = last[:, first : first + size]
        at += size
    common = at
    left_copy.wait()
    for c in range(3):
        for copy in copies[c]:
            copy.wait()
        if c == 0:
            begun_copy.wait()
        total = jnp.dot(rows[...], weights[c, :common], preferred_element_type=F32)
        final = total[early:]
        at = common
        for first, size in rest:
            final = final + jnp.dot(
                last[:, first : first + size], weights[c, at : at + size], preferred_element_type=F32
            )
            at += size
        parts = [(so_far[c] + total[:early]).astype(BF16), final.astype(BF16)]
        for n in range(early // BLK + 1):
            part, row = (parts[1], 0) if n * BLK == early else (parts[0], n * BLK)
            for h in range(heads):
                out[h, c, n] = part[row : row + BLK, h * HEAD_DIM : (h + 1) * HEAD_DIM]


def enter(flag, order, gain, begun, left, chunk, arrays, places, runs, rest, heads):
    features, width = chunk[0].shape[1], arrays[0].shape[2]
    early, common = left.shape
    smem = pl.BlockSpec(memory_space=pltpu.SMEM)
    vmem = pl.BlockSpec(memory_space=pltpu.VMEM)
    hbm = pl.BlockSpec(memory_space=pl.ANY)
    return pl.pallas_call(
        functools.partial(enter_kernel, heads, runs, rest, places),
        out_shape=jax.ShapeDtypeStruct((heads, 3, early // BLK + 1, BLK, HEAD_DIM), BF16),
        in_specs=[smem, smem, vmem] + [hbm] * (4 + len(arrays)),
        out_specs=vmem,
        scratch_shapes=[
            pltpu.VMEM((3, features, width), BF16),
            pltpu.VMEM((early + BLK, common), BF16),
            pltpu.VMEM((BLK, features), BF16),
            pltpu.VMEM(begun.shape, F32),
            pltpu.SemaphoreType.DMA((3,)),
            pltpu.SemaphoreType.DMA((3, len(arrays))),
        ],
        compiler_params=pltpu.CompilerParams(vmem_limit_bytes=58 << 20),
        cost_estimate=pl.CostEstimate(flops=1, bytes_accessed=1, transcendentals=0),
        name="enter",
    )(flag, order, gain, begun, left, *chunk, *arrays)


def leave_kernel(heads, lines, count, order, *refs):
    landed, pieces = refs[:2], refs[2 : 2 + 6 * count]
    outs = refs[2 + 6 * count : 4 + 6 * count]
    both, beside, rows, sems = refs[4 + 6 * count :]
    depth = heads * HEAD_DIM
    width = beside.shape[3]
    copies = []
    for kind in range(3):
        for core in range(2):
            at = 0
            for b in range(count):
                source = pieces[6 * b + 3 * core + kind]
                target = beside.at[kind - 1, core] if kind else both.at[core]
                copies.append(
                    pltpu.make_async_copy(source, target.at[pl.ds(at, source.shape[0])], sems.at[len(copies)])
                )
                copies[-1].start()
                at += source.shape[0]
    for side in range(2):
        for s in range(lines):
            for h in range(heads):
                at = s * depth + h * HEAD_DIM
                rows[side, :, at : at + HEAD_DIM] = landed[side][h * lines + order[s]]
    for kind in range(3):
        for core in range(2):
            for copy in copies[(kind * 2 + core) * count : (kind * 2 + core + 1) * count]:
                copy.wait()
            for side in range(2) if kind == 0 else (kind - 1,):
                weight = beside[kind - 1, core] if kind else both[core, :, side * width : (side + 1) * width]
                at = (2 * (kind > 0) + core) * width
                outs[side][:, at : at + width] = jnp.dot(
                    rows[side], weight, preferred_element_type=F32
                ).astype(BF16)


def leave(order, landed_x, landed_y, shared, heads, lines):
    depth = sum(batch[0].shape[0] for batch in shared)
    width = shared[0][0].shape[1] // 2
    arrays = [array for batch in shared for array in batch]
    smem = pl.BlockSpec(memory_space=pltpu.SMEM)
    vmem = pl.BlockSpec(memory_space=pltpu.VMEM)
    hbm = pl.BlockSpec(memory_space=pl.ANY)
    out = jax.ShapeDtypeStruct((BLK, 4 * width), BF16)
    return pl.pallas_call(
        functools.partial(leave_kernel, heads, lines, len(shared)),
        out_shape=(out, out),
        in_specs=[smem] + [vmem] * 2 + [hbm] * len(arrays),
        out_specs=(vmem, vmem),
        scratch_shapes=[
            pltpu.VMEM((2, depth, 2 * width), BF16),
            pltpu.VMEM((2, 2, depth, width), BF16),
            pltpu.VMEM((2, BLK, depth), BF16),
            pltpu.SemaphoreType.DMA((6 * len(shared),)),
        ],
        compiler_params=pltpu.CompilerParams(vmem_limit_bytes=48 << 20),
        cost_estimate=pl.CostEstimate(
            flops=16 * BLK * depth * width, bytes_accessed=16 * depth * width, transcendentals=0
        ),
        name="leave",
    )(order, landed_x, landed_y, *arrays)


def place_kernel(shifts, own_x, own_y, from_x, from_y, out):
    width = own_x.shape[1] // 4
    for ref, chips, half in ((own_x, (0, 2), 0), (own_y, (0, 1), 1), (from_x, (1, 3), 0), (from_y, (2, 3), 1)):
        for i, chip in enumerate(chips):
            for core in range(2):
                spot = ((shifts[0] ^ chip) * 2 + (shifts[1] ^ core)) * 2 + half
                at = (2 * i + core) * width
                out[:, pl.ds(pl.multiple_of(spot * width, width), width)] = ref[:, at : at + width]


def place(shifts, *parts):
    smem = pl.BlockSpec(memory_space=pltpu.SMEM)
    vmem = pl.BlockSpec(memory_space=pltpu.VMEM)
    return pl.pallas_call(
        place_kernel,
        out_shape=jax.ShapeDtypeStruct((BLK, 4 * parts[0].shape[1]), BF16),
        in_specs=[smem] + [vmem] * 4,
        out_specs=vmem,
        compiler_params=pltpu.CompilerParams(vmem_limit_bytes=16 << 20),
        name="place",
    )(shifts, *parts)


def by_head(projected):
    return lax.all_to_all(projected, "head", 0, 0, tiled=True)


def tables(heads, reps, lines, rep_at, order, layout, buckets):
    ints = jnp.int32

    def place_of(block):
        span = block // lines
        side = (span % reps) ^ rep_at if reps == 2 else span % reps
        slot = jnp.sum(jnp.where(block[..., None] % lines == order, jnp.arange(lines, dtype=ints), 0), axis=-1)
        return ((side * heads + span // reps) * 2) * lines + slot

    own = ((jnp.arange(heads, dtype=ints)[:, None] * reps + rep_at) * lines + order[None, :]).reshape(-1)
    listed = jnp.sum(
        jnp.where(own[:, None, None] == jnp.arange(layout.shape[0], dtype=ints)[None, :, None], layout[None], 0), axis=1
    )
    others = jnp.concatenate([(own - 1)[:, None], listed], axis=1)
    count = others.shape[1]
    at = jnp.arange(count, dtype=ints)
    mine = others == own[:, None]
    kept = (others >= 0) & ~mine
    same = (others[:, :, None] == others[:, None, :]) & kept[:, None, :]
    often = jnp.sum(same, axis=2)
    first = kept & ~jnp.any(same & (at[None, :] < at[:, None])[None], axis=2)
    rank = jnp.sum(first[:, None, :] & (at[None, :] < at[:, None])[None], axis=2)
    chosen = first[:, None, :] & (rank[:, None, :] == at[None, :, None])
    block = jnp.sum(jnp.where(chosen, others[:, None, :], 0), axis=2)
    times = jnp.sum(jnp.where(chosen, often[:, None, :], 0), axis=2)
    places = place_of(jnp.concatenate([own[:, None], jnp.where(times > 0, block, own[:, None])], axis=1))
    times = jnp.concatenate([1 + jnp.sum(mine, axis=1, keepdims=True), times], axis=1)
    biases = jnp.where(times > 0, jnp.log2(jnp.maximum(times, 1).astype(F32)), MASKED)
    distinct = jnp.sum(times > 0, axis=1)
    bucket = sum((distinct > size).astype(ints) for size in buckets[:-1])
    here = jnp.arange(own.shape[0], dtype=ints)
    ahead = (bucket[None, :] < bucket[:, None]) | ((bucket[None, :] == bucket[:, None]) & (here[None, :] < here[:, None]))
    turn = jnp.sum(ahead, axis=1)
    turns = jnp.sum(jnp.where(turn[None, :] == here[:, None], here[None, :], 0), axis=1)
    ends = jnp.sum(bucket[None, :] <= jnp.arange(len(buckets), dtype=ints)[:, None], axis=1)
    targets = (jnp.arange(heads, dtype=ints)[:, None] * lines + order[None, :]).reshape(-1)
    return places.astype(ints), biases, turns.astype(ints), ends.astype(ints), targets


def shards(heads, reps, lines, tokens, norm_gain, qkv_weight, out_weight, layout):
    head_at, rep_at, line_at = (lax.axis_index(a) for a in ("head", "rep", "line"))
    assert tokens.shape[0] == BLK
    order = jnp.asarray(line_order(lines), jnp.int32)[line_at]
    planes = plane_order(heads, head_at)
    fast = (heads, reps, lines) == (4, 2, 4)
    feature_order = jnp.stack(
        [(head_at ^ h) * reps + (rep_at ^ r) if fast else jnp.int32(h * reps + r) for r in range(reps) for h in range(heads)]
    ).astype(jnp.int32)
    planes = jnp.stack(planes).astype(jnp.int32)
    if fast:
        w_one, w_two = hop(qkv_weight, 1), hop(qkv_weight, 2)
    gain = norm_gain.reshape(1, -1)
    inside = (line_at == 1) | (line_at == 2)
    flag = jnp.where(inside, 0, 1).astype(jnp.int32).reshape(1)
    slots = 2 + layout.shape[1]
    buckets = sorted({min(8, slots), min(12, slots), slots})
    table = tables(heads, reps, lines, rep_at, order, layout, buckets)

    if not fast:
        weight = lax.all_gather(qkv_weight, ("head", "rep"), axis=1, tiled=True)
        rows = gathered(normalize(tokens, gain, feature_order), "line", lines)
        runs = [(0, weight.shape[1])]
        whole, _ = begin(flag, feature_order, gain, rows, [weight], runs, [], False)
        projected = whole.astype(BF16).reshape(3, lines, BLK, heads, HEAD_DIM).transpose(3, 0, 1, 2, 4)
        attended = attention(pair_gather(by_head(projected), reps), *table, buckets)
        landed = lax.all_to_all(attended, ("head", "line"), 0, 0, tiled=True)
        out_pieces = [
            (s, h, 0, piece)
            for s, part in enumerate(gathered(out_weight, "line", lines))
            for h, piece in enumerate(gathered(part, "head", heads))
        ]
        product = project(planes, order, pair_gather(landed, reps), out_pieces, heads, lines)
        columns = lax.all_to_all(product, "rep", 0, 0).reshape(reps, BLK, heads, -1)
        return columns.transpose(1, 2, 0, 3).reshape(BLK, -1)

    barrier = lax.optimization_barrier
    middle, outward, inward = [(1, 2), (2, 1)], [(1, 0), (2, 3)], [(0, 1), (3, 2)]

    def along(part, pairs):
        return lax.ppermute(part, "line", pairs)

    def pair(part):
        return lax.ppermute(part, "rep", xor_pairs(2, 1))

    def share(part):
        width = part.shape[1] // 2
        return hop(part[:, :width], 2), hop(part[:, width:], 1)

    near, across = along(tokens, xor_pairs(4, 1)), along(tokens, middle)
    w_others = [pair(qkv_weight)]
    near, across, w_others[0], *table = barrier((near, across, w_others[0], *table))
    second, crossed = along(across, outward), along(near, middle)
    half = qkv_weight.shape[1] // 2
    w_halves = [w_two[:, :half], w_one[:, half:]]
    o_halves = share(tie(out_weight, w_one, w_two))
    second, crossed, w_one, w_two, *halves = barrier((second, crossed, w_one, w_two, *w_halves, *o_halves))
    w_halves, o_halves = halves[:2], halves[2:]
    third = along(crossed, outward)
    w_first, w_other = hop(w_halves[0], 1), hop(w_halves[1], 2)
    w_others += [pair(w) for w in (w_one, w_two)]
    size = qkv_weight.shape[1]
    near_runs, far_runs = [(0, 3 * size), (4 * size, 3 * size)], [(3 * size, size), (7 * size, size)]
    chunks = [tokens, near, (across, second)]
    near_weights = [qkv_weight, w_one, w_two, *w_others]
    begun, left = begin(flag, feature_order, gain, chunks, near_weights, near_runs, far_runs, True)
    w_first, w_other, begun, left = barrier((w_first, w_other, begun, left))
    w_others = [pair(w) for w in (w_first, w_other)]
    third, o_own, *w_others = barrier((third, out_weight, *w_others))
    o_near, o_across = along(o_own, xor_pairs(4, 1)), along(o_own, middle)
    weights = [w_first, w_other, *w_others, *near_weights]
    places = [0, half, 2 * half, 3 * half] + [2 * size + i * size for i in range(6)]
    projected = enter(
        flag, feature_order, gain, begun, left, (crossed, third), weights, places, far_runs, near_runs, heads
    )
    projected, o_near, o_across = barrier((projected, o_near, o_across))
    mine = by_head(projected)
    o_crossed, o_second = along(o_near, middle), along(o_across, outward)
    mine, o_crossed, o_second = barrier((mine, o_crossed, o_second))
    o_third = along(o_crossed, outward)
    parts = pair_gather(mine, reps)
    batch = jnp.concatenate([o_near, jnp.where(inside, o_across, o_second)], axis=0)
    shared = [[out_weight, *o_halves], [batch, *share(batch)]]
    attended = attention(parts, *table, buckets)
    attended, o_third, *shared[1] = barrier((attended, o_third, *shared[1]))
    landed = lax.all_to_all(attended, ("head", "line"), 0, 0, tiled=True)
    last = jnp.where(inside, o_crossed, o_third)
    shared.append([last, *share(last)])
    landed, *rest = barrier((landed, *shared[2], *(pair(piece) for pieces in shared[:2] for piece in pieces)))
    shared = [shared[0] + rest[3:6], shared[1] + rest[6:]]
    landed_x, landed_y = hop(landed, 1), hop(landed, 2)
    shared.append(rest[:3] + [pair(piece) for piece in rest[:3]])
    own_x, own_y = leave(order, landed, landed, shared, heads, lines)
    own_x, own_y, landed_x, landed_y = barrier((own_x, own_y, landed_x, landed_y))
    to_x, to_y = leave(order, landed_x, landed_y, shared, heads, lines)
    shifts = jnp.stack([head_at, rep_at]).astype(jnp.int32)
    return place(shifts, own_x, own_y, hop(to_x, 1), hop(to_y, 2))


def solution(mesh):
    spans, lines = mesh.shape["ctx"], mesh.shape["fsdp"]

    def run(tokens, norm_gain, qkv_weight, out_weight, layout):
        heads = qkv_weight.shape[2] // lines // HEAD_DIM
        reps = spans // heads
        fine = Mesh(mesh.devices.reshape(heads, reps, lines), ("head", "rep", "line"))
        ctx = ("head", "rep")
        rows = P(("head", "rep", "line"), None)
        placed = (rows, P(), P(None, ctx, "line"), P("line", ctx), P())
        return jax.shard_map(
            functools.partial(shards, heads, reps, lines),
            mesh=fine,
            in_specs=placed,
            out_specs=rows,
            check_vma=False,
        )(tokens, norm_gain, qkv_weight, out_weight, layout)

    return run
```
